256 devices in a mesh: tau: 2 (over core), row: 8 (over y, z_hi), col: 16 (over z_lo, x).
Axes of the slice: x: 4, y: 4, z: 8 (z_hi: 2, z_lo: 4; z = z_hi * 4 + z_lo), core: 2. Of those that a mesh axis runs over, the one named last changes fastest.
Arguments:
- fock: bfloat16 [12288, 12288], P('row', 'col'), as said below
- green: bfloat16 [4, 12288, 12288], P('tau', 'row', 'col'), as said below
- factors: bfloat16 [4, 12288, 768], P('tau', ('row', 'col')), may hold values from -0.21875 to 0.21875
- tile_mask: int32 [48, 48], replicated, may hold values from 0 to 1, as said below
- start_block: float32 [12288, 512], P('col'), may hold values from -1.2 to 1.2
- lower_edge: float32 [1], replicated, may hold values from -1.3 to -0.7
- upper_edge: float32 [1], replicated, may hold values from 1.7 to 2.3
Outputs:
- filtered: float32 [12288, 512], P('row')
The draws below stay inside these ranges and needn't reach their ends.
Inputs may be any that keep to these rules, and one draw needn't show every extreme that they name: `fock`: symmetric. `green`: each of the 4 matrices is symmetric. `tile_mask`: symmetric, with every diagonal entry 1.
All inputs are finite; a program needn't handle non-finite values.
Results may differ from the reference program's by a relative error of at most 0.0072.
Values may be sent and summed in bfloat16 or wider, within the bound.
A program may use at most 128 MiB of HBM per device.

```python
import math
import jax
import jax.numpy as jnp
from jax import lax

N = 12288
SUB = 512
TILE = 256
K = 768
TAU_PTS = 4
NT = 48


def draw_fock(key, part):
    key = jax.random.fold_in(key, 11)
    base = jax.random.normal(key, (N, N), jnp.float32)
    return ((base + base.T) * (0.70710678 / math.sqrt(N))).astype(jnp.bfloat16)


def draw_green(key, part):
    key = jax.random.fold_in(key, 12)
    base = jax.random.normal(key, (TAU_PTS, N, N), jnp.float32)
    factor = 0.25 * 0.70710678 * math.sqrt(K / (N * TAU_PTS))
    return ((base + jnp.swapaxes(base, 1, 2)) * factor).astype(jnp.bfloat16)


def draw_tile_mask(key, part):
    key = jax.random.fold_in(key, 13)
    picks = jax.random.randint(key, (NT, NT), 0, 5)
    upper = (picks < 2).astype(jnp.int32)
    joined = jnp.maximum(upper, upper.T)
    positions = jnp.arange(NT, dtype=jnp.int32)
    return jnp.where(positions[:, None] == positions[None, :], 1, joined).astype(jnp.int32)


def levels(rng, shape, split, least, high):
    level, own = 1.0, jax.random.fold_in(rng, 6)
    for dim, blocks in split:
        steps = jnp.exp(jax.random.uniform(jax.random.fold_in(own, dim), (blocks,), jnp.float32, least / len(split), high / len(split)))
        level = level * jnp.repeat(steps, shape[dim] // blocks).reshape([-1 if axis == dim else 1 for axis in range(len(shape))])
    return level


def centred(rng, extent, scale, limit, pieces=(), held_as=jnp.bfloat16):
    level = levels(rng, extent, pieces, -0.22, 0.18) if pieces else 1.0
    result = jax.random.normal(rng, extent, jnp.float32) * scale * level
    return jnp.minimum(jnp.maximum(result, -limit), limit).astype(held_as)


def setup_inputs(seed: int = 0) -> dict:
    arg_keys = jax.random.split(jax.random.key(seed), 8)
    return {
        "fock": draw_fock(jax.random.fold_in(arg_keys[7], 71), 0),
        "green": draw_green(jax.random.fold_in(arg_keys[7], 71), 0),
        "factors": centred(arg_keys[2], (TAU_PTS, N, K), K ** -0.5, 0.21875, ((0, 2), (1, 128))),
        "tile_mask": draw_tile_mask(jax.random.fold_in(arg_keys[7], 71), 0),
        "start_block": centred(arg_keys[4], (N, SUB), 0.2, 1.2, ((0, 16),), jnp.float32),
        "lower_edge": jnp.clip(jax.random.uniform(arg_keys[5], (1,), jnp.float32, -1.3, -0.7), -1.3, -0.7),
        "upper_edge": jnp.clip(jax.random.uniform(arg_keys[6], (1,), jnp.float32, 1.7, 2.3), 1.7, 2.3),
    }


def reference(fock, green, factors, tile_mask, start_block, lower_edge, upper_edge):
    def add_point(tau_point, running):
        factor_rows = factors[tau_point]
        product = jnp.dot(factor_rows, factor_rows.T, preferred_element_type=jnp.float32)
        return running + product * green[tau_point].astype(jnp.float32)

    sigma = lax.fori_loop(0, TAU_PTS, add_point, jnp.zeros((N, N), jnp.float32))
    tile_count = N // TILE
    weights = tile_mask.astype(jnp.float32)
    sigma = (sigma.reshape(tile_count, TILE, tile_count, TILE) * weights[:, None, :, None]).reshape(N, N)
    center = 0.5 * (upper_edge[0] + lower_edge[0])
    half_width = 0.5 * (upper_edge[0] - lower_edge[0])
    positions = jnp.arange(N, dtype=jnp.int32)
    shifted = (fock.astype(jnp.float32) + sigma).at[positions, positions].add(-center)
    operator = (shifted / half_width).astype(jnp.bfloat16)
    first_block = jnp.dot(operator, start_block.astype(jnp.bfloat16), preferred_element_type=jnp.float32)
    second_block = 2.0 * jnp.dot(operator, first_block.astype(jnp.bfloat16), preferred_element_type=jnp.float32) - start_block
    filtered = 2.0 * jnp.dot(operator, second_block.astype(jnp.bfloat16), preferred_element_type=jnp.float32) - first_block
    return filtered
```

```python
import jax
import jax.numpy as jnp
from jax import lax
from jax.experimental import pallas as pl
from jax.experimental.pallas import tpu as pltpu
from jax.sharding import PartitionSpec as P

F32, BF16 = jnp.float32, jnp.bfloat16
NT = (((1,), (1,)), ((), ()))

PIECE = 96
SLAB = 384
BLOCK = 768
SUB = 512
TILE = 256
QUARTER = BLOCK // 4
SHARE = QUARTER // 4


def device(t, x, y, z):
    return (t, 2 * y + z // 4, 4 * (z % 4) + x)


def entry_y(x):
    return 2 * (1 - x % 2) + x // 2


def entry_x(y):
    return 2 * (y % 2) + 1 - y // 2


class Net:
    def __init__(self, send, recv):
        self.send, self.recv, self.count, self.started = send, recv, 0, []

    def put(self, src, dst, where):
        i = self.count
        self.count += 1
        copy = pltpu.make_async_remote_copy(
            src_ref=src, dst_ref=dst, send_sem=self.send.at[i], recv_sem=self.recv.at[i],
            device_id=where, device_id_type=pl.DeviceIdType.MESH,
        )
        copy.start()
        self.started.append(copy)
        return copy

    def drain(self):
        for copy in self.started:
            copy.wait_send()


class RingGather:
    def __init__(self, net, me, plus, minus, slot, source=None):
        self.net, self.me, self.plus, self.minus, self.slot = net, me, plus, minus, slot
        source = slot(me) if source is None else source
        self.up = net.put(source, slot(me), plus)
        self.down = net.put(source, slot(me), minus)

    def forward(self):
        before, after = (self.me + 3) % 4, (self.me + 1) % 4
        self.up.wait_recv()
        self.up2 = self.net.put(self.slot(before, 0), self.slot(before, 0), self.plus)
        self.down.wait_recv()
        self.down2 = self.net.put(self.slot(after, 1), self.slot(after, 1), self.minus)

    def finish(self):
        self.up2.wait_recv()
        self.down2.wait_recv()


def kernel(
    factors, green, fock, start, mask, lower, upper, out,
    frow, fcol, grn, fck, x0f, x0, sig, sgs, sgr, op, opt, part, stage, near, far, zin, zout,
    y1, y1own, part2, cstage, cin, stage2, near2, far2, hout, hin, y2, y3,
    send, recv, col_send, col_recv, local,
):
    t, r, c = lax.axis_index("tau"), lax.axis_index("row"), lax.axis_index("col")
    x, y, zl, zh = c % 4, r // 2, c // 4, r % 2
    z = 4 * zh + zl
    xp, xm = device(t, (x + 1) % 4, y, z), device(t, (x + 3) % 4, y, z)
    yp, ym = device(t, x, (y + 1) % 4, z), device(t, x, (y + 3) % 4, z)
    zls = (zl, zl + 1 - 2 * (zl % 2), (zl + 2) % 4, 3 - zl)
    zdev = [device(t, x, y, 4 * zh + s) for s in zls]
    hdev = device(t, x, y, 4 * (1 - zh) + zl)
    other = device(1 - t, x, y, z)
    targets = [device(t, z // 2, entry_y(x), y + 4 * h) for h in range(2)]
    sources = [device(t, entry_x(y), zl, 2 * x + e) for e in range(2)]

    barrier = pltpu.get_barrier_semaphore()
    greeted = [xp, xm, yp, ym, *zdev[1:], hdev, other, *targets, *sources]
    for where in greeted:
        pl.semaphore_signal(barrier, inc=1, device_id=where, device_id_type=pl.DeviceIdType.MESH)
    pl.semaphore_wait(barrier, len(greeted))

    net = Net(send, recv)

    def row_slot(slab):
        def slot(i, half=None):
            rows = pl.ds(pl.multiple_of(SLAB * slab + PIECE * i, 32), PIECE)
            return frow.at[:, rows, :] if half is None else frow.at[half, rows, :]
        return slot

    def col_slot(e):
        def slot(i, half=None):
            rows = pl.ds(pl.multiple_of(PIECE * (entry_x(i) + 4 * e), 32), PIECE)
            return fcol.at[:, rows, :] if half is None else fcol.at[half, rows, :]
        return slot

    own_col = fcol.at[:, pl.ds(pl.multiple_of(PIECE * (4 * (zl % 2) + x), 32), PIECE), :]
    col_out = [
        pltpu.make_async_remote_copy(
            src_ref=factors, dst_ref=own_col, send_sem=col_send.at[h], recv_sem=col_recv.at[zl % 2],
            device_id=targets[h], device_id_type=pl.DeviceIdType.MESH,
        )
        for h in range(2)
    ]
    for copy in col_out:
        copy.start()
    z_copies = [net.put(factors, row_slot(zl)(x), zdev[d]) for d in (1, 2, 3)]
    rings = [RingGather(net, x, xp, xm, row_slot(zl), factors)]

    own = pltpu.make_async_copy(factors, row_slot(zl)(x), local.at[0])
    own.start()
    load_green = pltpu.make_async_copy(green, grn, local.at[1])
    load_green.start()
    rows_t = pl.ds(pl.multiple_of(BLOCK * t, BLOCK), BLOCK)
    load_fock = pltpu.make_async_copy(fock.at[rows_t, :], fck, local.at[2])
    load_fock.start()
    load_start = pltpu.make_async_copy(start, x0f, local.at[3])
    load_start.start()

    z_copies[0].wait_recv()
    rings.append(RingGather(net, x, xp, xm, row_slot(zls[1])))
    cols = []
    for e in range(2):
        pltpu.make_async_remote_copy(
            src_ref=factors, dst_ref=own_col, send_sem=col_send.at[0], recv_sem=col_recv.at[e],
            device_id=targets[0], device_id_type=pl.DeviceIdType.MESH,
        ).wait_recv()
        cols.append(RingGather(net, y, yp, ym, col_slot(e)))
    rings[0].forward()
    z_copies[1].wait_recv()
    rings.append(RingGather(net, x, xp, xm, row_slot(zls[2])))
    rings[1].forward()
    z_copies[2].wait_recv()
    rings.append(RingGather(net, x, xp, xm, row_slot(zls[3])))
    for ring in cols:
        ring.forward()
    rings[2].forward()
    load_start.wait()
    x0[...] = x0f[...].astype(BF16)
    for ring in cols:
        ring.finish()

    load_green.wait()
    own.wait()

    def slab_sigma(slab):
        row0 = pl.multiple_of(SLAB * slab, 128)

        @pl.loop(0, BLOCK // TILE)
        def _(j):
            col0 = pl.multiple_of(TILE * j, TILE)
            total = jnp.zeros((SLAB, TILE), F32)
            for p in range(2):
                product = lax.dot_general(
                    frow[p, pl.ds(row0, SLAB), :], fcol[p, pl.ds(col0, TILE), :], NT, preferred_element_type=F32
                )
                total = total + product * grn[p, pl.ds(row0, SLAB), pl.ds(col0, TILE)].astype(F32)
            for b in range(SLAB // 128):
                keep = mask[6 * r + (3 * slab + b) // 2, 3 * c + j].astype(F32)
                sig[slab, pl.ds(128 * b, 128), pl.ds(col0, TILE)] = total[128 * b : 128 * (b + 1)] * keep

    def send_half():
        for u in range(2):
            sgs[u] = sig[2 * (1 - t) + u].astype(BF16)
            sig_out[u].start()

    sig_out = [
        pltpu.make_async_remote_copy(
            src_ref=sgs.at[u], dst_ref=sgr.at[u], send_sem=col_send.at[2 + u], recv_sem=col_recv.at[2 + u],
            device_id=other, device_id_type=pl.DeviceIdType.MESH,
        )
        for u in range(2)
    ]

    rings[0].finish()
    slab_sigma(zls[0])
    rings[1].finish()
    slab_sigma(zls[1])
    rings[3].forward()
    pl.when(zl // 2 != t)(send_half)
    rings[2].finish()
    slab_sigma(zls[2])
    rings[3].finish()
    slab_sigma(zls[3])
    pl.when(zl // 2 == t)(send_half)

    center = 0.5 * (upper[0] + lower[0])
    half_width = 0.5 * (upper[0] - lower[0])
    load_fock.wait()
    for u in range(2):
        sig_out[u].wait_recv()
        rows = pl.ds(SLAB * u, SLAB)
        shifted = fck[rows, :].astype(F32) + (sig[2 * t + u] + sgr[u].astype(F32))
        row_ids = lax.broadcasted_iota(jnp.int32, (SLAB, BLOCK), 0) + (2 * BLOCK * r + BLOCK * t + SLAB * u)
        col_ids = lax.broadcasted_iota(jnp.int32, (SLAB, BLOCK), 1) + BLOCK * c
        shifted = jnp.where(row_ids == col_ids, shifted - center, shifted)
        op[rows, :] = (shifted / half_width).astype(BF16)

    def ring_reduce(me, plus, minus, size, partial_rows, stage, near, far):
        h = size // 2

        def rows(i, half):
            return pl.ds(pl.multiple_of(size * i + h * half, 16), h)

        a, b, opposite = (me + 1) % 4, (me + 3) % 4, (me + 2) % 4
        stage[pl.ds(pl.multiple_of(size * opposite, 32), size), :] = partial_rows(opposite).astype(BF16)
        far_up = net.put(stage.at[rows(opposite, 0), :], far.at[0], plus)
        far_down = net.put(stage.at[rows(opposite, 1), :], far.at[1], minus)
        va = partial_rows(a)
        stage[rows(a, 1), :] = va[h:].astype(BF16)
        up1 = net.put(stage.at[rows(a, 1), :], near.at[1], plus)
        vb = partial_rows(b)
        stage[rows(b, 0), :] = vb[:h].astype(BF16)
        down0 = net.put(stage.at[rows(b, 0), :], near.at[2], minus)
        mine = partial_rows(me)
        far_up.wait_recv()
        stage[rows(a, 0), :] = (va[:h] + far[0].astype(F32)).astype(BF16)
        up0 = net.put(stage.at[rows(a, 0), :], near.at[0], plus)
        far_down.wait_recv()
        stage[rows(b, 1), :] = (vb[h:] + far[1].astype(F32)).astype(BF16)
        down1 = net.put(stage.at[rows(b, 1), :], near.at[3], minus)
        for copy in (up1, down0, up0, down1):
            copy.wait_recv()
        first = mine[:h] + near[0].astype(F32) + near[2].astype(F32)
        second = mine[h:] + near[1].astype(F32) + near[3].astype(F32)
        return first, second

    def across(block, n):
        def partial_rows(i):
            at = pl.ds(pl.multiple_of(QUARTER * i, 64), QUARTER)
            part[at, :] = jnp.dot(op[at, :], block[...], preferred_element_type=F32)
            return part[at, :]

        first, second = ring_reduce(x, xp, xm, QUARTER, partial_rows, stage.at[n], near.at[n], far.at[n])
        for i, half in enumerate((first, second)):
            part[pl.ds(2 * SHARE * i, 2 * SHARE), :] = half
            zout[n, pl.ds(2 * SHARE * i, 2 * SHARE), :] = half.astype(BF16)

        def share(s):
            return pl.ds(pl.multiple_of(SHARE * s, 16), SHARE)

        copies = [net.put(zout.at[n, share(zls[d]), :], zin.at[n, d - 1], zdev[d]) for d in (1, 2, 3)]
        total = part[share(zl), :]
        for d in (1, 2, 3):
            copies[d - 1].wait_recv()
            total = total + zin[n, d - 1].astype(F32)
        return total

    def gather_rows(buffer):
        def slots(s):
            def slot(i, half=None):
                rows = pl.ds(pl.multiple_of(QUARTER * i + SHARE * s, 16), SHARE)
                return buffer.at[rows, :] if half is None else buffer.at[rows, pl.ds(SUB // 2 * half, SUB // 2)]
            return slot

        here = slots(zl)(x)
        zc = [net.put(here, here, zdev[d]) for d in (1, 2, 3)]
        rings = [RingGather(net, x, xp, xm, slots(zl))]
        for d in (1, 2, 3):
            zc[d - 1].wait_recv()
            rings.append(RingGather(net, x, xp, xm, slots(zls[d])))
        for ring in rings:
            ring.forward()
        for ring in rings:
            ring.finish()

    my_share = pl.ds(pl.multiple_of(QUARTER * x + SHARE * zl, 16), SHARE)

    total = across(x0, 0)
    y1own[...] = total
    y1[my_share, :] = total.astype(BF16)
    for i in range(3):
        for j in range(3):
            opt[pl.ds(TILE * j, TILE), pl.ds(TILE * i, TILE)] = op[pl.ds(TILE * i, TILE), pl.ds(TILE * j, TILE)].T
    gather_rows(y1)

    far_half = pl.ds(pl.multiple_of(SLAB * (1 - t), SLAB), SLAB)
    near_half = pl.ds(pl.multiple_of(SLAB * t, SLAB), SLAB)
    cstage[...] = jnp.dot(opt[far_half, :], y1[...], preferred_element_type=F32).astype(BF16)
    swap = net.put(cstage, cin, other)
    part2[...] = jnp.dot(opt[near_half, :], y1[...], preferred_element_type=F32)
    swap.wait_recv()
    part2[...] = part2[...] + cin[...].astype(F32)
    shard = SLAB // 4

    def rows2(i):
        return part2[pl.ds(pl.multiple_of(shard * i, 32), shard), :]

    first, second = ring_reduce(y, yp, ym, shard, rows2, stage2, near2, far2)
    total = jnp.concatenate([first, second], axis=0)
    hout[...] = total.astype(BF16)
    over = net.put(hout, hin, hdev)
    over.wait_recv()
    total = total + hin[...].astype(F32)

    def slot2(i, half=None):
        rows = pl.ds(pl.multiple_of(SLAB * t + shard * i, 32), shard)
        return y2.at[rows, :] if half is None else y2.at[rows, pl.ds(SUB // 2 * half, SUB // 2)]

    mine2 = pl.ds(pl.multiple_of(SLAB * t + shard * y, 32), shard)
    y2[mine2, :] = (2.0 * total - x0f[mine2, :]).astype(BF16)
    ring = RingGather(net, y, yp, ym, slot2)
    ring.forward()
    ring.finish()
    both = net.put(y2.at[near_half, :], y2.at[near_half, :], other)
    both.wait_recv()

    total = across(y2, 1)
    here = pl.ds(pl.multiple_of(BLOCK * t + QUARTER * x + SHARE * zl, 16), SHARE)
    y3[here, :] = (2.0 * total - y1own[...]).astype(BF16)
    gather_rows(y3.at[rows_t, :])
    last = net.put(y3.at[rows_t, :], y3.at[rows_t, :], other)
    store = pltpu.make_async_copy(y3.at[rows_t, :], out.at[rows_t, :], local.at[4])
    store.start()
    last.wait_recv()
    rows_o = pl.ds(pl.multiple_of(BLOCK * (1 - t), BLOCK), BLOCK)
    store2 = pltpu.make_async_copy(y3.at[rows_o, :], out.at[rows_o, :], local.at[5])
    store2.start()
    for copy in col_out + sig_out:
        copy.wait_send()
    net.drain()
    store.wait()
    store2.wait()


def on_device(fock, green, factors, tile_mask, start_block, lower_edge, upper_edge):
    anywhere, smem = pl.BlockSpec(memory_space=pl.ANY), pl.BlockSpec(memory_space=pltpu.SMEM)
    v = pltpu.VMEM
    q2, s2 = QUARTER // 2, SLAB // 8
    result = pl.pallas_call(
        kernel,
        out_shape=jax.ShapeDtypeStruct((2 * BLOCK, SUB), BF16),
        in_specs=[anywhere] * 4 + [smem] * 3,
        out_specs=anywhere,
        scratch_shapes=[
            v((2, 2 * BLOCK, 768), BF16),
            v((2, BLOCK, 768), BF16),
            v((2, 2 * BLOCK, BLOCK), BF16),
            v((BLOCK, BLOCK), BF16),
            v((BLOCK, SUB), F32),
            v((BLOCK, SUB), BF16),
            v((4, SLAB, BLOCK), F32),
            v((2, SLAB, BLOCK), BF16),
            v((2, SLAB, BLOCK), BF16),
            v((BLOCK, BLOCK), BF16),
            v((BLOCK, BLOCK), BF16),
            v((BLOCK, SUB), F32),
            v((2, BLOCK, SUB), BF16),
            v((2, 4, q2, SUB), BF16),
            v((2, 2, q2, SUB), BF16),
            v((2, 3, SHARE, SUB), BF16),
            v((2, QUARTER, SUB), BF16),
            v((BLOCK, SUB), BF16),
            v((SHARE, SUB), F32),
            v((SLAB, SUB), F32),
            v((SLAB, SUB), BF16),
            v((SLAB, SUB), BF16),
            v((SLAB, SUB), BF16),
            v((4, s2, SUB), BF16),
            v((2, s2, SUB), BF16),
            v((2 * s2, SUB), BF16),
            v((2 * s2, SUB), BF16),
            v((BLOCK, SUB), BF16),
            v((2 * BLOCK, SUB), BF16),
            pltpu.SemaphoreType.DMA((112,)),
            pltpu.SemaphoreType.DMA((112,)),
            pltpu.SemaphoreType.DMA((4,)),
            pltpu.SemaphoreType.DMA((4,)),
            pltpu.SemaphoreType.DMA((6,)),
        ],
        compiler_params=pltpu.CompilerParams(
            collective_id=0, has_side_effects=True, vmem_limit_bytes=56 * 2**20
        ),
        name="filter_kernel",
    )(factors, green, fock, start_block, tile_mask, lower_edge, upper_edge)
    return result.astype(F32)


def solution(mesh):
    placed = (
        P("row", "col"),
        P("tau", "row", "col"),
        P("tau", ("row", "col"), None),
        P(),
        P("col", None),
        P(),
        P(),
    )
    return jax.shard_map(
        on_device, mesh=mesh, in_specs=placed, out_specs=P("row", None), check_vma=False
    )
```

```python
import jax
import jax.numpy as jnp
from jax import lax
from jax.experimental import pallas as pl
from jax.experimental.pallas import tpu as pltpu
from jax.sharding import PartitionSpec as P

F32, BF16 = jnp.float32, jnp.bfloat16
NT = (((1,), (1,)), ((), ()))

PIECE = 96
SLAB = 384
BLOCK = 768
SUB = 512
PARTS = 2
W = SUB // PARTS
COPIES = 28 + 70 * PARTS
TILE = 256
QUARTER = BLOCK // 4
SHARE = QUARTER // 4


def device(t, x, y, z):
    return (t, 2 * y + z // 4, 4 * (z % 4) + x)


class Net:
    def __init__(self, send, recv):
        self.send, self.recv, self.count, self.started = send, recv, 0, []

    def put(self, src, dst, where):
        i = self.count
        self.count += 1
        copy = pltpu.make_async_remote_copy(
            src_ref=src, dst_ref=dst, send_sem=self.send.at[i], recv_sem=self.recv.at[i],
            device_id=where, device_id_type=pl.DeviceIdType.MESH,
        )
        copy.start()
        self.started.append(copy)
        return copy

    def drain(self):
        assert self.count == COPIES
        for copy in self.started:
            copy.wait_send()


class RingGather:
    def __init__(self, net, me, plus, minus, slot, source=None):
        self.net, self.me, self.plus, self.minus, self.slot = net, me, plus, minus, slot
        source = slot(me) if source is None else source
        self.up = net.put(source, slot(me), plus)
        self.down = net.put(source, slot(me), minus)

    def forward(self):
        before, after = (self.me + 3) % 4, (self.me + 1) % 4
        self.up.wait_recv()
        self.up2 = self.net.put(self.slot(before, 0), self.slot(before, 0), self.plus)
        self.down.wait_recv()
        self.down2 = self.net.put(self.slot(after, 1), self.slot(after, 1), self.minus)

    def finish(self):
        self.up2.wait_recv()
        self.down2.wait_recv()


class Send:
    def __init__(self, src, dst, send_sem, recv_sem, where, is_self):
        self.is_self = is_self
        self.remote = pltpu.make_async_remote_copy(
            src_ref=src, dst_ref=dst, send_sem=send_sem, recv_sem=recv_sem,
            device_id=where, device_id_type=pl.DeviceIdType.MESH,
        )
        self.local = pltpu.make_async_copy(src, dst, recv_sem)

    def start(self):
        pl.when(self.is_self)(lambda: self.local.start())
        pl.when(jnp.logical_not(self.is_self))(lambda: self.remote.start())

    def wait_send(self):
        pl.when(jnp.logical_not(self.is_self))(lambda: self.remote.wait_send())


def in_turn(*tasks):
    tasks = list(tasks)
    while tasks:
        for task in list(tasks):
            try:
                next(task)
            except StopIteration:
                tasks.remove(task)


def kernel(
    factors, green, fock, start, mask, lower, upper, out,
    frow, fcol, fy, fz, grn, fck, x0f, x0, sig, sgs, sgr, op, opt, part, stage, near, far, zin, zout,
    y1, y1own, part2, cstage, cin, stage2, near2, far2, hout, hin, y2, y3,
    send, recv, z_send, z_recv, cy_send, cy_recv, cz_send, cz_recv, cx_send, cx_recv, sig_send, sig_recv, local,
):
    t, r, c = lax.axis_index("tau"), lax.axis_index("row"), lax.axis_index("col")
    x, y, zl, zh = c % 4, r // 2, c // 4, r % 2
    z = 4 * zh + zl
    xp, xm = device(t, (x + 1) % 4, y, z), device(t, (x + 3) % 4, y, z)
    yp, ym = device(t, x, (y + 1) % 4, z), device(t, x, (y + 3) % 4, z)
    zls = (zl, zl + 1 - 2 * (zl % 2), (zl + 2) % 4, 3 - zl)
    zdev = [device(t, x, y, 4 * zh + s) for s in zls]
    hdev = device(t, x, y, 4 * (1 - zh) + zl)
    other = device(1 - t, x, y, z)

    def by_zl(*values):
        return jnp.where(zl == 0, values[0], jnp.where(zl == 1, values[1], jnp.where(zl == 2, values[2], values[3])))

    slabs = (zl, by_zl(1, 0, 3, 2), by_zl(2, 2, 1, 1), by_zl(3, 3, 0, 0))

    entry = (x + y + z) % 4
    home_y = (y - x - z + 12) % 4
    source_z = (y - x - zl + 8) % 4
    to_x = [source_z // 2 + 2 * h for h in range(2)]

    def entry_x(at_y, e):
        return (at_y - zl - 2 * x - e + 12) % 4

    def along(i, j, k):
        return device(t, i, j, k), (i == x) & (j == y) & (k == z)

    y_to, y_from = along(x, entry, z), along(x, home_y, z)
    z_to = [along(x, y, home_y + 4 * h) for h in range(2)]
    z_from = [along(x, y, source_z + 4 * h) for h in range(2)]
    x_to = [along(to_x[h], y, z) for h in range(2)]
    x_from = [along(entry_x(y, e), y, z) for e in range(2)]

    rows_t = pl.ds(pl.multiple_of(BLOCK * t, BLOCK), BLOCK)
    load_green = pltpu.make_async_copy(green, grn, local.at[1])
    load_fock = pltpu.make_async_copy(fock.at[rows_t, :], fck, local.at[2])
    load_start = pltpu.make_async_copy(start, x0f, local.at[3])

    barrier = pltpu.get_barrier_semaphore()
    greeted = [xp, xm, yp, ym, *zdev[1:], hdev, other]
    greeted += [where for where, _ in [y_to, y_from] + z_to + z_from + x_to + x_from]
    for where in greeted:
        pl.semaphore_signal(barrier, inc=1, device_id=where, device_id_type=pl.DeviceIdType.MESH)
    pl.semaphore_wait(barrier, len(greeted))

    net = Net(send, recv)

    def row_slot(slab):
        def slot(i, half=None):
            rows = pl.ds(pl.multiple_of(SLAB * slab + PIECE * i, 32), PIECE)
            return frow.at[:, rows, :] if half is None else frow.at[half, rows, :]
        return slot

    def col_rows(e, from_x):
        return pl.ds(pl.multiple_of(PIECE * (4 * e + from_x), 32), PIECE)

    def col_slot(e):
        def slot(i, half=None):
            rows = col_rows(e, entry_x(i, e))
            return fcol.at[:, rows, :] if half is None else fcol.at[half, rows, :]
        return slot

    sends = []

    def go(src, dst, send_sem, recv_sem, target):
        copy = Send(src, dst, send_sem, recv_sem, *target)
        copy.start()
        sends.append(copy)

    def arrived(dst, recv_sem):
        pltpu.make_async_copy(dst, dst, recv_sem).wait()

    def along_z(source, slab, condition, where, i):
        copy = pltpu.make_async_remote_copy(
            src_ref=source, dst_ref=row_slot(slab)(x), send_sem=z_send.at[i], recv_sem=z_recv.at[slab],
            device_id=where, device_id_type=pl.DeviceIdType.MESH,
        )
        pl.when(condition)(lambda: copy.start())
        z_sent.append((condition, copy))

    z_sent = []
    z_up, z_down = device(t, x, y, 4 * zh + (zl + 1) % 4), device(t, x, y, 4 * zh + (zl + 3) % 4)
    along_z(factors, zl, zl < 3, z_up, 0)
    along_z(factors, zl, zl > 0, z_down, 1)
    for p in range(2):
        go(factors.at[p], fy.at[p], cy_send.at[p], cy_recv.at[p], y_to)
    rings = [RingGather(net, x, xp, xm, row_slot(zl), factors)]
    own = pltpu.make_async_copy(factors, row_slot(zl)(x), local.at[0])
    own.start()
    load_green.start()
    load_fock.start()
    load_start.start()

    def next_slab(k):
        slab = slabs[k]
        slot = row_slot(slab)(x)
        arrived(slot, z_recv.at[slab])
        up = slab < zl
        where = device(t, x, y, 4 * zh + jnp.where(up, (zl + 1) % 4, (zl + 3) % 4))
        along_z(slot, slab, jnp.where(up, zl < 3, zl > 0), where, 1 + k)
        rings.append(RingGather(net, x, xp, xm, row_slot(slab)))

    def cols_z(p):
        arrived(fy.at[p], cy_recv.at[p])
        for h in range(2):
            go(fy.at[p], fz.at[zh, p], cz_send.at[2 * h + p], cz_recv.at[2 * zh + p], z_to[h])

    def cols_x(p):
        e = source_z % 2
        for h in range(2):
            arrived(fz.at[h, p], cz_recv.at[2 * h + p])
            go(fz.at[h, p], fcol.at[p, col_rows(e, x), :], cx_send.at[2 * h + p], cx_recv.at[2 * e + p], x_to[h])

    col_up, col_down = {}, {}

    def cols_y(p):
        for e in range(2):
            mine = col_slot(e)(y, p)
            arrived(mine, cx_recv.at[2 * e + p])
            col_up[e, p] = net.put(mine, mine, yp)
            col_down[e, p] = net.put(mine, mine, ym)

    def cols_forward(p):
        copies = []
        for e in range(2):
            first, neighbour, where = (col_up[e, p], (y + 3) % 4, yp) if p == 0 else (col_down[e, p], (y + 1) % 4, ym)
            first.wait_recv()
            passed = col_slot(e)(neighbour, p)
            copies.append(net.put(passed, passed, where))
        return copies

    cols_z(0)
    next_slab(1)
    cols_z(1)
    cols_x(0)
    rings[0].forward()
    cols_x(1)
    cols_y(0)
    next_slab(2)
    rings[1].forward()
    cols_y(1)
    next_slab(3)
    far_cols = cols_forward(0) + cols_forward(1)
    rings[2].forward()
    rings[3].forward()
    load_start.wait()
    for p in range(PARTS):
        x0[p] = x0f[:, W * p : W * (p + 1)].astype(BF16)
    for e in range(2):
        col_up[e, 1].wait_recv()
        col_down[e, 0].wait_recv()
    for copy in far_cols:
        copy.wait_recv()

    load_green.wait()
    load_fock.wait()
    own.wait()

    def sig_copy(u):
        return pltpu.make_async_remote_copy(
            src_ref=sgs.at[u], dst_ref=sgr.at[u], send_sem=sig_send.at[u], recv_sem=sig_recv.at[u],
            device_id=other, device_id_type=pl.DeviceIdType.MESH,
        )

    def slab_sigma(slab):
        row0 = pl.multiple_of(SLAB * slab, 128)

        @pl.loop(0, BLOCK // TILE)
        def _(j):
            col0 = pl.multiple_of(TILE * j, TILE)
            total = jnp.zeros((SLAB, TILE), F32)
            for p in range(2):
                product = lax.dot_general(
                    frow[p, pl.ds(row0, SLAB), :], fcol[p, pl.ds(col0, TILE), :], NT, preferred_element_type=F32
                )
                total = total + product * grn[p, pl.ds(row0, SLAB), pl.ds(col0, TILE)].astype(F32)
            for b in range(SLAB // 128):
                keep = mask[6 * r + (3 * slab + b) // 2, 3 * c + j].astype(F32)
                sig[slab, pl.ds(128 * b, 128), pl.ds(col0, TILE)] = total[128 * b : 128 * (b + 1)] * keep

        @pl.when(slab // 2 != t)
        def _():
            sgs[slab % 2] = sig[slab].astype(BF16)
            sig_copy(slab % 2).start()

    center = 0.5 * (upper[0] + lower[0])
    half_width = 0.5 * (upper[0] - lower[0])

    def make_operator(which):
        for slab in which:
            u = slab % 2
            sig_copy(u).wait_recv()
            rows = pl.ds(pl.multiple_of(SLAB * u, 128), SLAB)
            shifted = fck[rows, :].astype(F32) + (sig[slab] + sgr[u].astype(F32))
            row_ids = lax.broadcasted_iota(jnp.int32, (SLAB, BLOCK), 0) + (2 * BLOCK * r + SLAB * slab)
            col_ids = lax.broadcasted_iota(jnp.int32, (SLAB, BLOCK), 1) + BLOCK * c
            shifted = jnp.where(row_ids == col_ids, shifted - center, shifted)
            op[rows, :] = (shifted / half_width).astype(BF16)

    rings[0].finish()
    slab_sigma(slabs[0])
    rings[1].finish()
    slab_sigma(slabs[1])
    pl.when(zl // 2 == t)(lambda: make_operator(slabs[:2]))
    rings[2].finish()
    slab_sigma(slabs[2])
    rings[3].finish()
    slab_sigma(slabs[3])
    pl.when(zl // 2 != t)(lambda: make_operator(slabs[2:]))

    def ring_reduce(me, plus, minus, size, ready, part, stage, near, far):
        h = size // 2

        def rows(i, half):
            return pl.ds(pl.multiple_of(size * i + h * half, 16), h)

        def push(i, half, there, where):
            return net.put(stage.at[rows(i, half), :], there, where)

        a, b, opposite = (me + 1) % 4, (me + 3) % 4, (me + 2) % 4
        ready(opposite)
        for half in range(2):
            stage[rows(opposite, half), :] = part[rows(opposite, half), :].astype(BF16)
        far_up = push(opposite, 0, far.at[0], plus)
        far_down = push(opposite, 1, far.at[1], minus)
        ready(a)
        stage[rows(a, 1), :] = part[rows(a, 1), :].astype(BF16)
        up1 = push(a, 1, near.at[1], plus)
        ready(b)
        stage[rows(b, 0), :] = part[rows(b, 0), :].astype(BF16)
        down0 = push(b, 0, near.at[2], minus)
        ready(me)
        yield
        far_up.wait_recv()
        stage[rows(a, 0), :] = (part[rows(a, 0), :] + far[0].astype(F32)).astype(BF16)
        up0 = push(a, 0, near.at[0], plus)
        far_down.wait_recv()
        stage[rows(b, 1), :] = (part[rows(b, 1), :] + far[1].astype(F32)).astype(BF16)
        down1 = push(b, 1, near.at[3], minus)
        yield
        for copy in (up1, down0, up0, down1):
            copy.wait_recv()
        for half in range(2):
            at = rows(me, half)
            part[at, :] = part[at, :] + near[half].astype(F32) + near[2 + half].astype(F32)

    def across(block, n, p):
        prt = part.at[p]

        def ready(i):
            at = pl.ds(pl.multiple_of(QUARTER * i, 64), QUARTER)
            prt[at, :] = jnp.dot(op[at, :], block[...], preferred_element_type=F32)

        k = PARTS * n + p
        yield from ring_reduce(x, xp, xm, QUARTER, ready, prt, stage.at[k], near.at[k], far.at[k])
        zout[k] = prt[pl.ds(pl.multiple_of(QUARTER * x, 64), QUARTER), :].astype(BF16)

        def share(s):
            return pl.ds(pl.multiple_of(SHARE * s, 16), SHARE)

        copies = [net.put(zout.at[k, share(zls[d]), :], zin.at[k, d - 1], zdev[d]) for d in (1, 2, 3)]
        yield
        total = prt[pl.ds(pl.multiple_of(QUARTER * x + SHARE * zl, 16), SHARE), :]
        for d in (1, 2, 3):
            copies[d - 1].wait_recv()
            total = total + zin[k, d - 1].astype(F32)
        return total

    def gather_rows(buffer):
        def slots(s):
            def slot(i, half=None):
                rows = pl.ds(pl.multiple_of(QUARTER * i + SHARE * s, 16), SHARE)
                return buffer.at[rows, :] if half is None else buffer.at[rows, pl.ds(W // 2 * half, W // 2)]
            return slot

        here = slots(zl)(x)
        zc = [net.put(here, here, zdev[d]) for d in (1, 2, 3)]
        rings = [RingGather(net, x, xp, xm, slots(zl))]
        yield
        for d in (1, 2, 3):
            zc[d - 1].wait_recv()
            rings.append(RingGather(net, x, xp, xm, slots(zls[d])))
        yield
        for ring in rings:
            ring.forward()
        yield
        for ring in rings:
            ring.finish()

    far_half = pl.ds(pl.multiple_of(SLAB * (1 - t), SLAB), SLAB)
    near_half = pl.ds(pl.multiple_of(SLAB * t, SLAB), SLAB)
    rows_o = pl.ds(pl.multiple_of(BLOCK * (1 - t), BLOCK), BLOCK)
    my_share = pl.ds(pl.multiple_of(QUARTER * x + SHARE * zl, 16), SHARE)
    my_out = pl.ds(pl.multiple_of(BLOCK * t + QUARTER * x + SHARE * zl, 16), SHARE)
    shard = SLAB // 4
    my_shard = pl.ds(pl.multiple_of(shard * y, 32), shard)
    mine2 = pl.ds(pl.multiple_of(SLAB * t + shard * y, 32), shard)
    stores = []

    def transpose():
        yield
        for i in range(3):
            for j in range(3):
                opt[pl.ds(TILE * j, TILE), pl.ds(TILE * i, TILE)] = op[pl.ds(TILE * i, TILE), pl.ds(TILE * j, TILE)].T

    def steps(p):
        cols = pl.ds(W * p, W)
        total = yield from across(x0.at[p], 0, p)
        y1own[p] = total
        y1[p, my_share, :] = total.astype(BF16)
        yield from gather_rows(y1.at[p])

        cstage[p] = jnp.dot(opt[far_half, :], y1[p], preferred_element_type=F32).astype(BF16)
        swap = net.put(cstage.at[p], cin.at[p], other)
        part2[p] = jnp.dot(opt[near_half, :], y1[p], preferred_element_type=F32)
        swap.wait_recv()
        part2[p] = part2[p] + cin[p].astype(F32)
        yield from ring_reduce(
            y, yp, ym, shard, lambda i: None, part2.at[p], stage2.at[p], near2.at[p], far2.at[p]
        )
        hout[p] = part2[p, my_shard, :].astype(BF16)
        over = net.put(hout.at[p], hin.at[p], hdev)
        yield
        over.wait_recv()
        total = part2[p, my_shard, :] + hin[p].astype(F32)

        def slot2(i, half=None):
            rows = pl.ds(pl.multiple_of(SLAB * t + shard * i, 32), shard)
            return y2.at[p, rows, :] if half is None else y2.at[p, rows, pl.ds(W // 2 * half, W // 2)]

        y2[p, mine2, :] = (2.0 * total - x0f[mine2, cols]).astype(BF16)
        ring = RingGather(net, y, yp, ym, slot2)
        yield
        ring.forward()
        yield
        ring.finish()
        both = net.put(y2.at[p, near_half, :], y2.at[p, near_half, :], other)
        yield
        both.wait_recv()

        total = yield from across(y2.at[p], 1, p)
        y3[p, my_out, :] = (2.0 * total - y1own[p]).astype(BF16)
        yield from gather_rows(y3.at[p, rows_t, :])
        last = net.put(y3.at[p, rows_t, :], y3.at[p, rows_t, :], other)
        stores.append(pltpu.make_async_copy(y3.at[p, rows_t, :], out.at[rows_t, cols], local.at[4 + 2 * p]))
        stores[-1].start()
        yield
        last.wait_recv()
        stores.append(pltpu.make_async_copy(y3.at[p, rows_o, :], out.at[rows_o, cols], local.at[5 + 2 * p]))
        stores[-1].start()

    in_turn(*[steps(p) for p in range(PARTS)], transpose())

    for copy in sends:
        copy.wait_send()
    for condition, copy in z_sent:
        pl.when(condition)(lambda: copy.wait_send())
    for u in range(2):
        sig_copy(u).wait_send()
    net.drain()
    for copy in stores:
        copy.wait()


def on_device(fock, green, factors, tile_mask, start_block, lower_edge, upper_edge):
    anywhere, smem = pl.BlockSpec(memory_space=pl.ANY), pl.BlockSpec(memory_space=pltpu.SMEM)
    v, dma = pltpu.VMEM, pltpu.SemaphoreType.DMA
    q2, s2 = QUARTER // 2, SLAB // 8
    result = pl.pallas_call(
        kernel,
        out_shape=jax.ShapeDtypeStruct((2 * BLOCK, SUB), BF16),
        in_specs=[anywhere] * 4 + [smem] * 3,
        out_specs=anywhere,
        scratch_shapes=[
            v((2, 2 * BLOCK, 768), BF16),
            v((2, BLOCK, 768), BF16),
            v((2, PIECE, 768), BF16),
            v((2, 2, PIECE, 768), BF16),
            v((2, 2 * BLOCK, BLOCK), BF16),
            v((BLOCK, BLOCK), BF16),
            v((BLOCK, SUB), F32),
            v((PARTS, BLOCK, W), BF16),
            v((4, SLAB, BLOCK), F32),
            v((2, SLAB, BLOCK), BF16),
            v((2, SLAB, BLOCK), BF16),
            v((BLOCK, BLOCK), BF16),
            v((BLOCK, BLOCK), BF16),
            v((PARTS, BLOCK, W), F32),
            v((2 * PARTS, BLOCK, W), BF16),
            v((2 * PARTS, 4, q2, W), BF16),
            v((2 * PARTS, 2, q2, W), BF16),
            v((2 * PARTS, 3, SHARE, W), BF16),
            v((2 * PARTS, QUARTER, W), BF16),
            v((PARTS, BLOCK, W), BF16),
            v((PARTS, SHARE, W), F32),
            v((PARTS, SLAB, W), F32),
            v((PARTS, SLAB, W), BF16),
            v((PARTS, SLAB, W), BF16),
            v((PARTS, SLAB, W), BF16),
            v((PARTS, 4, s2, W), BF16),
            v((PARTS, 2, s2, W), BF16),
            v((PARTS, 2 * s2, W), BF16),
            v((PARTS, 2 * s2, W), BF16),
            v((PARTS, BLOCK, W), BF16),
            v((PARTS, 2 * BLOCK, W), BF16),
            dma((COPIES,)),
            dma((COPIES,)),
            dma((5,)),
            dma((4,)),
            dma((2,)),
            dma((2,)),
            dma((4,)),
            dma((4,)),
            dma((4,)),
            dma((4,)),
            dma((2,)),
            dma((2,)),
            dma((4 + 2 * PARTS,)),
        ],
        compiler_params=pltpu.CompilerParams(
            collective_id=0, has_side_effects=True, vmem_limit_bytes=56 * 2**20
        ),
        name="filter_kernel",
    )(factors, green, fock, start_block, tile_mask, lower_edge, upper_edge)
    return result.astype(F32)


def solution(mesh):
    placed = (
        P("row", "col"),
        P("tau", "row", "col"),
        P("tau", ("row", "col"), None),
        P(),
        P("col", None),
        P(),
        P(),
    )
    return jax.shard_map(
        on_device, mesh=mesh, in_specs=placed, out_specs=P("row", None), check_vma=False
    )
```

```python
import jax
import jax.numpy as jnp
from jax import lax
from jax.experimental import pallas as pl
from jax.experimental.pallas import tpu as pltpu
from jax.sharding import PartitionSpec as P

F32, BF16 = jnp.float32, jnp.bfloat16
NT = (((1,), (1,)), ((), ()))

PIECE = 96
CHUNK = PIECE // 2
SLAB = 384
BLOCK = 768
SUB = 512
PARTS = 2
W = SUB // PARTS
COPIES = 40 + 66 * PARTS
TILE = 256
QUARTER = BLOCK // 4
SHARE = QUARTER // 4


def device(t, x, y, z):
    return (t, 2 * y + z // 4, 4 * (z % 4) + x)


class Net:
    def __init__(self, send, recv):
        self.send, self.recv, self.count, self.started = send, recv, 0, []

    def put(self, src, dst, where):
        i = self.count
        self.count += 1
        copy = pltpu.make_async_remote_copy(
            src_ref=src, dst_ref=dst, send_sem=self.send.at[i], recv_sem=self.recv.at[i],
            device_id=where, device_id_type=pl.DeviceIdType.MESH,
        )
        copy.start()
        self.started.append(copy)
        return copy

    def drain(self):
        assert self.count == COPIES
        for copy in self.started:
            copy.wait_send()


class RingGather:
    def __init__(self, net, me, plus, minus, slot, source=None):
        self.net, self.me, self.plus, self.minus, self.slot = net, me, plus, minus, slot
        source = slot(me) if source is None else source
        self.up = net.put(source, slot(me), plus)
        self.down = net.put(source, slot(me), minus)

    def forward(self):
        before, after = (self.me + 3) % 4, (self.me + 1) % 4
        self.up.wait_recv()
        self.up2 = self.net.put(self.slot(before, 0), self.slot(before, 0), self.plus)
        self.down.wait_recv()
        self.down2 = self.net.put(self.slot(after, 1), self.slot(after, 1), self.minus)

    def finish(self):
        self.up2.wait_recv()
        self.down2.wait_recv()


class DirectGather:
    def __init__(self, net, me, plus, minus, opposite, slot):
        mine = slot(me)
        self.copies = [net.put(mine, mine, where) for where in (opposite, plus, minus)]

    def finish(self):
        for copy in self.copies:
            copy.wait_recv()


class Send:
    def __init__(self, src, dst, send_sem, recv_sem, where, is_self):
        self.is_self = is_self
        self.remote = pltpu.make_async_remote_copy(
            src_ref=src, dst_ref=dst, send_sem=send_sem, recv_sem=recv_sem,
            device_id=where, device_id_type=pl.DeviceIdType.MESH,
        )
        self.local = pltpu.make_async_copy(src, dst, recv_sem)

    def start(self):
        pl.when(self.is_self)(lambda: self.local.start())
        pl.when(jnp.logical_not(self.is_self))(lambda: self.remote.start())

    def wait_send(self):
        pl.when(jnp.logical_not(self.is_self))(lambda: self.remote.wait_send())


def in_turn(*tasks):
    tasks = list(tasks)
    while tasks:
        for task in list(tasks):
            try:
                next(task)
            except StopIteration:
                tasks.remove(task)


def kernel(
    factors, green, fock, start, mask, lower, upper, out,
    frow, fcol, fy, fz, grn, fck, x0f, x0, sig, sgs, sgr, op, opt, part, stage, near, far, zin, zout,
    y1, y1own, part2, cstage, cin, stage2, near2, far2, hout, hin, y2, y3,
    send, recv, z_send, z_recv, cy_send, cy_recv, cz_send, cz_recv, cx_send, cx_recv, sig_send, sig_recv, local,
):
    t, r, c = lax.axis_index("tau"), lax.axis_index("row"), lax.axis_index("col")
    x, y, zl, zh = c % 4, r // 2, c // 4, r % 2
    z = 4 * zh + zl
    xp, xm = device(t, (x + 1) % 4, y, z), device(t, (x + 3) % 4, y, z)
    yp, ym = device(t, x, (y + 1) % 4, z), device(t, x, (y + 3) % 4, z)
    yo = device(t, x, (y + 2) % 4, z)
    zls = (zl, zl + 1 - 2 * (zl % 2), (zl + 2) % 4, 3 - zl)
    zdev = [device(t, x, y, 4 * zh + s) for s in zls]
    hdev = device(t, x, y, 4 * (1 - zh) + zl)
    other = device(1 - t, x, y, z)

    def by_zl(*values):
        return jnp.where(zl == 0, values[0], jnp.where(zl == 1, values[1], jnp.where(zl == 2, values[2], values[3])))

    slabs = (zl, by_zl(1, 0, 3, 2), by_zl(2, 2, 1, 1), by_zl(3, 3, 0, 0))

    entry = (x + y + z) % 4
    home_y = (y - x - z + 12) % 4
    source_z = (y - x - zl + 8) % 4
    to_x = [source_z // 2 + 2 * h for h in range(2)]

    def entry_x(at_y, e):
        return (at_y - zl - 2 * x - e + 12) % 4

    def along(i, j, k):
        return device(t, i, j, k), (i == x) & (j == y) & (k == z)

    y_to, y_from = along(x, entry, z), along(x, home_y, z)
    z_to = [along(x, y, home_y + 4 * h) for h in range(2)]
    z_from = [along(x, y, source_z + 4 * h) for h in range(2)]
    x_to = [along(to_x[h], y, z) for h in range(2)]
    x_from = [along(entry_x(y, e), y, z) for e in range(2)]

    rows_t = pl.ds(pl.multiple_of(BLOCK * t, BLOCK), BLOCK)
    load_green = pltpu.make_async_copy(green, grn, local.at[1])
    load_fock = pltpu.make_async_copy(fock.at[rows_t, :], fck, local.at[2])
    load_start = pltpu.make_async_copy(start, x0f, local.at[3])

    barrier = pltpu.get_barrier_semaphore()
    greeted = [xp, xm, yp, ym, yo, *zdev[1:], hdev, other]
    greeted += [where for where, _ in [y_to, y_from] + z_to + z_from + x_to + x_from]
    for where in greeted:
        pl.semaphore_signal(barrier, inc=1, device_id=where, device_id_type=pl.DeviceIdType.MESH)
    pl.semaphore_wait(barrier, len(greeted))

    net = Net(send, recv)

    def row_slot(slab):
        def slot(i, half=None):
            rows = pl.ds(pl.multiple_of(SLAB * slab + PIECE * i, 32), PIECE)
            return frow.at[:, rows, :] if half is None else frow.at[half, rows, :]
        return slot

    def chunk(ref, q, first=0):
        return ref.at[q // 2, pl.ds(pl.multiple_of(first + CHUNK * (q % 2), 16), CHUNK), :]

    def col_slot(e, from_x, q):
        return chunk(fcol, q, PIECE * (4 * e + from_x))

    sends = []

    def go(src, dst, send_sem, recv_sem, target):
        copy = Send(src, dst, send_sem, recv_sem, *target)
        copy.start()
        sends.append(copy)

    def arrived(dst, recv_sem):
        pltpu.make_async_copy(dst, dst, recv_sem).wait()

    def along_z(source, slab, condition, where, i):
        copy = pltpu.make_async_remote_copy(
            src_ref=source, dst_ref=row_slot(slab)(x), send_sem=z_send.at[i], recv_sem=z_recv.at[slab],
            device_id=where, device_id_type=pl.DeviceIdType.MESH,
        )
        pl.when(condition)(lambda: copy.start())
        z_sent.append((condition, copy))

    z_sent = []
    z_up, z_down = device(t, x, y, 4 * zh + (zl + 1) % 4), device(t, x, y, 4 * zh + (zl + 3) % 4)
    along_z(factors, zl, zl < 3, z_up, 0)
    along_z(factors, zl, zl > 0, z_down, 1)
    for q in range(4):
        go(chunk(factors, q), chunk(fy, q), cy_send.at[q], cy_recv.at[q], y_to)
    rings = [RingGather(net, x, xp, xm, row_slot(zl), factors)]
    own = pltpu.make_async_copy(factors, row_slot(zl)(x), local.at[0])
    own.start()
    load_green.start()
    load_fock.start()
    load_start.start()

    def next_slab(k):
        slab = slabs[k]
        slot = row_slot(slab)(x)
        arrived(slot, z_recv.at[slab])
        up = slab < zl
        where = device(t, x, y, 4 * zh + jnp.where(up, (zl + 1) % 4, (zl + 3) % 4))
        along_z(slot, slab, jnp.where(up, zl < 3, zl > 0), where, 1 + k)
        rings.append(RingGather(net, x, xp, xm, row_slot(slab)))

    def cols_z(q):
        arrived(chunk(fy, q), cy_recv.at[q])
        for h in range(2):
            go(chunk(fy, q), chunk(fz.at[zh], q), cz_send.at[4 * h + q], cz_recv.at[4 * zh + q], z_to[h])

    def cols_x(q):
        e = source_z % 2
        for h in range(2):
            arrived(chunk(fz.at[h], q), cz_recv.at[4 * h + q])
            go(chunk(fz.at[h], q), col_slot(e, x, q), cx_send.at[4 * h + q], cx_recv.at[4 * e + q], x_to[h])

    col_up, col_down, far_cols = {}, {}, []

    def cols_y(q):
        for e in range(2):
            mine = col_slot(e, entry_x(y, e), q)
            arrived(mine, cx_recv.at[4 * e + q])
            col_up[e, q] = net.put(mine, mine, yp)
            col_down[e, q] = net.put(mine, mine, ym)

    def cols_forward(q):
        for e in range(2):
            first, neighbour, where = (col_down[e, q], (y + 1) % 4, ym) if q % 2 else (col_up[e, q], (y + 3) % 4, yp)
            first.wait_recv()
            passed = col_slot(e, entry_x(neighbour, e), q)
            far_cols.append(net.put(passed, passed, where))

    for q in range(4):
        cols_z(q)
    rings[0].forward()
    next_slab(1)
    cols_x(0)
    cols_x(1)
    cols_y(0)
    cols_x(2)
    cols_y(1)
    cols_x(3)
    rings[1].forward()
    next_slab(2)
    cols_y(2)
    cols_forward(0)
    cols_y(3)
    cols_forward(1)
    next_slab(3)
    rings[2].forward()
    cols_forward(2)
    cols_forward(3)
    rings[3].forward()
    load_start.wait()
    for p in range(PARTS):
        x0[p] = x0f[:, W * p : W * (p + 1)].astype(BF16)
    for e in range(2):
        for q in range(4):
            (col_up if q % 2 else col_down)[e, q].wait_recv()
    for copy in far_cols:
        copy.wait_recv()

    load_green.wait()
    load_fock.wait()
    own.wait()

    def sig_copy(u):
        return pltpu.make_async_remote_copy(
            src_ref=sgs.at[u], dst_ref=sgr.at[u], send_sem=sig_send.at[u], recv_sem=sig_recv.at[u],
            device_id=other, device_id_type=pl.DeviceIdType.MESH,
        )

    def slab_sigma(slab):
        row0 = pl.multiple_of(SLAB * slab, 128)

        @pl.loop(0, BLOCK // TILE)
        def _(j):
            col0 = pl.multiple_of(TILE * j, TILE)
            total = jnp.zeros((SLAB, TILE), F32)
            for p in range(2):
                product = lax.dot_general(
                    frow[p, pl.ds(row0, SLAB), :], fcol[p, pl.ds(col0, TILE), :], NT, preferred_element_type=F32
                )
                total = total + product * grn[p, pl.ds(row0, SLAB), pl.ds(col0, TILE)].astype(F32)
            for b in range(SLAB // 128):
                keep = mask[6 * r + (3 * slab + b) // 2, 3 * c + j].astype(F32)
                sig[slab, pl.ds(128 * b, 128), pl.ds(col0, TILE)] = total[128 * b : 128 * (b + 1)] * keep

        @pl.when(slab // 2 != t)
        def _():
            sgs[slab % 2] = sig[slab].astype(BF16)
            sig_copy(slab % 2).start()

    center = 0.5 * (upper[0] + lower[0])
    half_width = 0.5 * (upper[0] - lower[0])

    def make_operator(which):
        for slab in which:
            u = slab % 2
            sig_copy(u).wait_recv()
            rows = pl.ds(pl.multiple_of(SLAB * u, 128), SLAB)
            shifted = fck[rows, :].astype(F32) + (sig[slab] + sgr[u].astype(F32))
            row_ids = lax.broadcasted_iota(jnp.int32, (SLAB, BLOCK), 0) + (2 * BLOCK * r + SLAB * slab)
            col_ids = lax.broadcasted_iota(jnp.int32, (SLAB, BLOCK), 1) + BLOCK * c
            shifted = jnp.where(row_ids == col_ids, shifted - center, shifted)
            op[rows, :] = (shifted / half_width).astype(BF16)

    rings[0].finish()
    slab_sigma(slabs[0])
    rings[1].finish()
    slab_sigma(slabs[1])
    pl.when(zl // 2 == t)(lambda: make_operator(slabs[:2]))
    rings[2].finish()
    slab_sigma(slabs[2])
    rings[3].finish()
    slab_sigma(slabs[3])
    pl.when(zl // 2 != t)(lambda: make_operator(slabs[2:]))

    def direct_reduce(me, plus, minus, opposite, size, ready, part, stage, near, far):
        def rows(i):
            return pl.ds(pl.multiple_of(size * i, 32), size)

        copies = []
        for k, where, into in ((2, opposite, far), (1, plus, near.at[0]), (3, minus, near.at[1])):
            at = rows((me + k) % 4)
            ready((me + k) % 4)
            stage[at, :] = part[at, :].astype(BF16)
            copies.append(net.put(stage.at[at, :], into, where))
        ready(me)
        yield
        for copy in copies:
            copy.wait_recv()
        at = rows(me)
        part[at, :] = part[at, :] + far[...].astype(F32) + (near[0].astype(F32) + near[1].astype(F32))

    def ring_reduce(me, plus, minus, size, ready, part, stage, near, far):
        h = size // 2

        def rows(i, half):
            return pl.ds(pl.multiple_of(size * i + h * half, 16), h)

        def push(i, half, there, where):
            return net.put(stage.at[rows(i, half), :], there, where)

        a, b, opposite = (me + 1) % 4, (me + 3) % 4, (me + 2) % 4
        ready(opposite)
        for half in range(2):
            stage[rows(opposite, half), :] = part[rows(opposite, half), :].astype(BF16)
        far_up = push(opposite, 0, far.at[0], plus)
        far_down = push(opposite, 1, far.at[1], minus)
        ready(a)
        stage[rows(a, 1), :] = part[rows(a, 1), :].astype(BF16)
        up1 = push(a, 1, near.at[1], plus)
        ready(b)
        stage[rows(b, 0), :] = part[rows(b, 0), :].astype(BF16)
        down0 = push(b, 0, near.at[2], minus)
        ready(me)
        yield
        far_up.wait_recv()
        stage[rows(a, 0), :] = (part[rows(a, 0), :] + far[0].astype(F32)).astype(BF16)
        up0 = push(a, 0, near.at[0], plus)
        far_down.wait_recv()
        stage[rows(b, 1), :] = (part[rows(b, 1), :] + far[1].astype(F32)).astype(BF16)
        down1 = push(b, 1, near.at[3], minus)
        yield
        for copy in (up1, down0, up0, down1):
            copy.wait_recv()
        for half in range(2):
            at = rows(me, half)
            part[at, :] = part[at, :] + near[half].astype(F32) + near[2 + half].astype(F32)

    def across(block, n, p):
        prt = part.at[p]

        def ready(i):
            at = pl.ds(pl.multiple_of(QUARTER * i, 64), QUARTER)
            prt[at, :] = jnp.dot(op[at, :], block[...], preferred_element_type=F32)

        k = PARTS * n + p
        yield from ring_reduce(x, xp, xm, QUARTER, ready, prt, stage.at[k], near.at[k], far.at[k])
        zout[k] = prt[pl.ds(pl.multiple_of(QUARTER * x, 64), QUARTER), :].astype(BF16)

        def share(s):
            return pl.ds(pl.multiple_of(SHARE * s, 16), SHARE)

        copies = [net.put(zout.at[k, share(zls[d]), :], zin.at[k, d - 1], zdev[d]) for d in (1, 2, 3)]
        yield
        total = prt[pl.ds(pl.multiple_of(QUARTER * x + SHARE * zl, 16), SHARE), :]
        for d in (1, 2, 3):
            copies[d - 1].wait_recv()
            total = total + zin[k, d - 1].astype(F32)
        return total

    def gather_rows(buffer):
        def slots(s):
            def slot(i, half=None):
                rows = pl.ds(pl.multiple_of(QUARTER * i + SHARE * s, 16), SHARE)
                return buffer.at[rows, :] if half is None else buffer.at[rows, pl.ds(W // 2 * half, W // 2)]
            return slot

        here = slots(zl)(x)
        zc = [net.put(here, here, zdev[d]) for d in (1, 2, 3)]
        rings = [RingGather(net, x, xp, xm, slots(zl))]
        yield
        for d in (1, 2, 3):
            zc[d - 1].wait_recv()
            rings.append(RingGather(net, x, xp, xm, slots(zls[d])))
        yield
        for ring in rings:
            ring.forward()
        yield
        for ring in rings:
            ring.finish()

    far_half = pl.ds(pl.multiple_of(SLAB * (1 - t), SLAB), SLAB)
    near_half = pl.ds(pl.multiple_of(SLAB * t, SLAB), SLAB)
    rows_o = pl.ds(pl.multiple_of(BLOCK * (1 - t), BLOCK), BLOCK)
    my_share = pl.ds(pl.multiple_of(QUARTER * x + SHARE * zl, 16), SHARE)
    my_out = pl.ds(pl.multiple_of(BLOCK * t + QUARTER * x + SHARE * zl, 16), SHARE)
    shard = SLAB // 4
    my_shard = pl.ds(pl.multiple_of(shard * y, 32), shard)
    mine2 = pl.ds(pl.multiple_of(SLAB * t + shard * y, 32), shard)
    stores = []

    def transpose():
        yield
        for i in range(3):
            for j in range(3):
                opt[pl.ds(TILE * j, TILE), pl.ds(TILE * i, TILE)] = op[pl.ds(TILE * i, TILE), pl.ds(TILE * j, TILE)].T

    def steps(p):
        cols = pl.ds(W * p, W)
        total = yield from across(x0.at[p], 0, p)
        y1own[p] = total
        y1[p, my_share, :] = total.astype(BF16)
        yield from gather_rows(y1.at[p])

        cstage[p] = jnp.dot(opt[far_half, :], y1[p], preferred_element_type=F32).astype(BF16)
        swap = net.put(cstage.at[p], cin.at[p], other)
        part2[p] = jnp.dot(opt[near_half, :], y1[p], preferred_element_type=F32)
        swap.wait_recv()
        part2[p] = part2[p] + cin[p].astype(F32)
        yield from direct_reduce(
            y, yp, ym, yo, shard, lambda i: None, part2.at[p], stage2.at[p], near2.at[p], far2.at[p]
        )
        hout[p] = part2[p, my_shard, :].astype(BF16)
        over = net.put(hout.at[p], hin.at[p], hdev)
        yield
        over.wait_recv()
        total = part2[p, my_shard, :] + hin[p].astype(F32)

        def slot2(i, half=None):
            rows = pl.ds(pl.multiple_of(SLAB * t + shard * i, 32), shard)
            return y2.at[p, rows, :] if half is None else y2.at[p, rows, pl.ds(W // 2 * half, W // 2)]

        y2[p, mine2, :] = (2.0 * total - x0f[mine2, cols]).astype(BF16)
        ring = DirectGather(net, y, yp, ym, yo, slot2)
        yield
        ring.finish()
        both = net.put(y2.at[p, near_half, :], y2.at[p, near_half, :], other)
        yield
        both.wait_recv()

        total = yield from across(y2.at[p], 1, p)
        y3[p, my_out, :] = (2.0 * total - y1own[p]).astype(BF16)
        yield from gather_rows(y3.at[p, rows_t, :])
        last = net.put(y3.at[p, rows_t, :], y3.at[p, rows_t, :], other)
        stores.append(pltpu.make_async_copy(y3.at[p, rows_t, :], out.at[rows_t, cols], local.at[4 + 2 * p]))
        stores[-1].start()
        yield
        last.wait_recv()
        stores.append(pltpu.make_async_copy(y3.at[p, rows_o, :], out.at[rows_o, cols], local.at[5 + 2 * p]))
        stores[-1].start()

    in_turn(*[steps(p) for p in range(PARTS)], transpose())

    for copy in sends:
        copy.wait_send()
    for condition, copy in z_sent:
        pl.when(condition)(lambda: copy.wait_send())
    for u in range(2):
        sig_copy(u).wait_send()
    net.drain()
    for copy in stores:
        copy.wait()


def on_device(fock, green, factors, tile_mask, start_block, lower_edge, upper_edge):
    anywhere, smem = pl.BlockSpec(memory_space=pl.ANY), pl.BlockSpec(memory_space=pltpu.SMEM)
    v, dma = pltpu.VMEM, pltpu.SemaphoreType.DMA
    q2, s2 = QUARTER // 2, SLAB // 8
    result = pl.pallas_call(
        kernel,
        out_shape=jax.ShapeDtypeStruct((2 * BLOCK, SUB), BF16),
        in_specs=[anywhere] * 4 + [smem] * 3,
        out_specs=anywhere,
        scratch_shapes=[
            v((2, 2 * BLOCK, 768), BF16),
            v((2, BLOCK, 768), BF16),
            v((2, PIECE, 768), BF16),
            v((2, 2, PIECE, 768), BF16),
            v((2, 2 * BLOCK, BLOCK), BF16),
            v((BLOCK, BLOCK), BF16),
            v((BLOCK, SUB), F32),
            v((PARTS, BLOCK, W), BF16),
            v((4, SLAB, BLOCK), F32),
            v((2, SLAB, BLOCK), BF16),
            v((2, SLAB, BLOCK), BF16),
            v((BLOCK, BLOCK), BF16),
            v((BLOCK, BLOCK), BF16),
            v((PARTS, BLOCK, W), F32),
            v((2 * PARTS, BLOCK, W), BF16),
            v((2 * PARTS, 4, q2, W), BF16),
            v((2 * PARTS, 2, q2, W), BF16),
            v((2 * PARTS, 3, SHARE, W), BF16),
            v((2 * PARTS, QUARTER, W), BF16),
            v((PARTS, BLOCK, W), BF16),
            v((PARTS, SHARE, W), F32),
            v((PARTS, SLAB, W), F32),
            v((PARTS, SLAB, W), BF16),
            v((PARTS, SLAB, W), BF16),
            v((PARTS, SLAB, W), BF16),
            v((PARTS, 2, 2 * s2, W), BF16),
            v((PARTS, 2 * s2, W), BF16),
            v((PARTS, 2 * s2, W), BF16),
            v((PARTS, 2 * s2, W), BF16),
            v((PARTS, BLOCK, W), BF16),
            v((PARTS, 2 * BLOCK, W), BF16),
            dma((COPIES,)),
            dma((COPIES,)),
            dma((5,)),
            dma((4,)),
            dma((4,)),
            dma((4,)),
            dma((8,)),
            dma((8,)),
            dma((8,)),
            dma((8,)),
            dma((2,)),
            dma((2,)),
            dma((4 + 2 * PARTS,)),
        ],
        compiler_params=pltpu.CompilerParams(
            collective_id=0, has_side_effects=True, vmem_limit_bytes=52 * 2**20
        ),
        name="filter_kernel",
    )(factors, green, fock, start_block, tile_mask, lower_edge, upper_edge)
    return result.astype(F32)


def solution(mesh):
    placed = (
        P("row", "col"),
        P("tau", "row", "col"),
        P("tau", ("row", "col"), None),
        P(),
        P("col", None),
        P(),
        P(),
    )
    return jax.shard_map(
        on_device, mesh=mesh, in_specs=placed, out_specs=P("row", None), check_vma=False
    )
```

```python
import jax
import jax.numpy as jnp
from jax import lax
from jax.experimental import pallas as pl
from jax.experimental.pallas import tpu as pltpu
from jax.sharding import PartitionSpec as P

F32, BF16 = jnp.float32, jnp.bfloat16
NT = (((1,), (1,)), ((), ()))

PIECE = 96
CHUNK = PIECE // 2
SLAB = 384
BLOCK = 768
SUB = 512
PARTS = 2
W = SUB // PARTS
COPIES = 48 + 66 * PARTS
TILE = 256
QUARTER = BLOCK // 4
SHARE = QUARTER // 4


def device(t, x, y, z):
    return (t, 2 * y + z // 4, 4 * (z % 4) + x)


class Net:
    def __init__(self, send, recv):
        self.send, self.recv, self.count, self.started = send, recv, 0, []

    def put(self, src, dst, where):
        i = self.count
        self.count += 1
        copy = pltpu.make_async_remote_copy(
            src_ref=src, dst_ref=dst, send_sem=self.send.at[i], recv_sem=self.recv.at[i],
            device_id=where, device_id_type=pl.DeviceIdType.MESH,
        )
        copy.start()
        self.started.append(copy)
        return copy

    def drain(self):
        assert self.count == COPIES
        for copy in self.started:
            copy.wait_send()


class RingGather:
    def __init__(self, net, me, plus, minus, slot, source=None):
        self.net, self.me, self.plus, self.minus, self.slot = net, me, plus, minus, slot
        source = slot(me) if source is None else source
        self.up = net.put(source, slot(me), plus)
        self.down = net.put(source, slot(me), minus)

    def forward(self):
        before, after = (self.me + 3) % 4, (self.me + 1) % 4
        self.up.wait_recv()
        self.up2 = self.net.put(self.slot(before, 0), self.slot(before, 0), self.plus)
        self.down.wait_recv()
        self.down2 = self.net.put(self.slot(after, 1), self.slot(after, 1), self.minus)

    def finish(self):
        self.up2.wait_recv()
        self.down2.wait_recv()


class SplitRingGather(RingGather):
    def __init__(self, net, me, plus, minus, slot, source=None):
        self.net, self.me, self.plus, self.minus, self.slot = net, me, plus, minus, slot

        def half(h, where):
            src = slot(me, h) if source is None else source.at[h]
            return net.put(src, slot(me, h), where)

        self.up, self.down = half(0, plus), half(1, minus)
        self.rest = [half(1, plus), half(0, minus)]

    def finish(self):
        for copy in self.rest:
            copy.wait_recv()
        super().finish()


class DirectGather:
    def __init__(self, net, me, plus, minus, opposite, slot):
        mine = slot(me)
        self.copies = [net.put(mine, mine, where) for where in (opposite, plus, minus)]

    def finish(self):
        for copy in self.copies:
            copy.wait_recv()


class Send:
    def __init__(self, src, dst, send_sem, recv_sem, where, is_self):
        self.is_self = is_self
        self.remote = pltpu.make_async_remote_copy(
            src_ref=src, dst_ref=dst, send_sem=send_sem, recv_sem=recv_sem,
            device_id=where, device_id_type=pl.DeviceIdType.MESH,
        )
        self.local = pltpu.make_async_copy(src, dst, recv_sem)

    def start(self):
        pl.when(self.is_self)(lambda: self.local.start())
        pl.when(jnp.logical_not(self.is_self))(lambda: self.remote.start())

    def wait_send(self):
        pl.when(jnp.logical_not(self.is_self))(lambda: self.remote.wait_send())


def in_turn(*tasks):
    tasks = list(tasks)
    while tasks:
        for task in list(tasks):
            try:
                next(task)
            except StopIteration:
                tasks.remove(task)


def kernel(
    factors, green, fock, start, mask, lower, upper, out,
    frow, fcol, fy, fz, grn, fck, x0f, x0, sig, sgs, sgr, op, opt, part, stage, near, far, zin, zout,
    y1, y1own, part2, cstage, cin, stage2, near2, far2, hout, hin, y2, y3,
    send, recv, z_send, z_recv, cy_send, cy_recv, cz_send, cz_recv, cx_send, cx_recv, sig_send, sig_recv, local,
):
    t, r, c = lax.axis_index("tau"), lax.axis_index("row"), lax.axis_index("col")
    x, y, zl, zh = c % 4, r // 2, c // 4, r % 2
    z = 4 * zh + zl
    xp, xm = device(t, (x + 1) % 4, y, z), device(t, (x + 3) % 4, y, z)
    yp, ym = device(t, x, (y + 1) % 4, z), device(t, x, (y + 3) % 4, z)
    yo = device(t, x, (y + 2) % 4, z)
    zls = (zl, zl + 1 - 2 * (zl % 2), (zl + 2) % 4, 3 - zl)
    zdev = [device(t, x, y, 4 * zh + s) for s in zls]
    hdev = device(t, x, y, 4 * (1 - zh) + zl)
    other = device(1 - t, x, y, z)

    def by_zl(*values):
        return jnp.where(zl == 0, values[0], jnp.where(zl == 1, values[1], jnp.where(zl == 2, values[2], values[3])))

    slabs = (zl, by_zl(1, 0, 3, 2), by_zl(2, 2, 1, 1), by_zl(3, 3, 0, 0))

    entry = (x + y + z) % 4
    home_y = (y - x - z + 12) % 4
    source_z = (y - x - zl + 8) % 4
    to_x = [source_z // 2 + 2 * h for h in range(2)]

    def entry_x(at_y, e):
        return (at_y - zl - 2 * x - e + 12) % 4

    def along(i, j, k):
        return device(t, i, j, k), (i == x) & (j == y) & (k == z)

    y_to, y_from = along(x, entry, z), along(x, home_y, z)
    z_to = [along(x, y, home_y + 4 * h) for h in range(2)]
    z_from = [along(x, y, source_z + 4 * h) for h in range(2)]
    x_to = [along(to_x[h], y, z) for h in range(2)]
    x_from = [along(entry_x(y, e), y, z) for e in range(2)]

    rows_t = pl.ds(pl.multiple_of(BLOCK * t, BLOCK), BLOCK)
    load_green = pltpu.make_async_copy(green, grn, local.at[1])
    load_fock = pltpu.make_async_copy(fock.at[rows_t, :], fck, local.at[2])
    load_start = pltpu.make_async_copy(start, x0f, local.at[3])

    barrier = pltpu.get_barrier_semaphore()
    greeted = [xp, xm, yp, ym, yo, *zdev[1:], hdev, other]
    greeted += [where for where, _ in [y_to, y_from] + z_to + z_from + x_to + x_from]
    for where in greeted:
        pl.semaphore_signal(barrier, inc=1, device_id=where, device_id_type=pl.DeviceIdType.MESH)
    pl.semaphore_wait(barrier, len(greeted))

    net = Net(send, recv)

    def row_slot(slab):
        def slot(i, half=None):
            rows = pl.ds(pl.multiple_of(SLAB * slab + PIECE * i, 32), PIECE)
            return frow.at[:, rows, :] if half is None else frow.at[half, rows, :]
        return slot

    def chunk(ref, q, first=0):
        return ref.at[q // 2, pl.ds(pl.multiple_of(first + CHUNK * (q % 2), 16), CHUNK), :]

    def col_slot(e, from_x, q):
        return chunk(fcol, q, PIECE * (4 * e + from_x))

    sends = []

    def go(src, dst, send_sem, recv_sem, target):
        copy = Send(src, dst, send_sem, recv_sem, *target)
        copy.start()
        sends.append(copy)

    def arrived(dst, recv_sem):
        pltpu.make_async_copy(dst, dst, recv_sem).wait()

    def along_z(source, slab, condition, where, i):
        copy = pltpu.make_async_remote_copy(
            src_ref=source, dst_ref=row_slot(slab)(x), send_sem=z_send.at[i], recv_sem=z_recv.at[slab],
            device_id=where, device_id_type=pl.DeviceIdType.MESH,
        )
        pl.when(condition)(lambda: copy.start())
        z_sent.append((condition, copy))

    z_sent = []
    z_up, z_down = device(t, x, y, 4 * zh + (zl + 1) % 4), device(t, x, y, 4 * zh + (zl + 3) % 4)
    along_z(factors, zl, zl < 3, z_up, 0)
    along_z(factors, zl, zl > 0, z_down, 1)
    for q in range(4):
        go(chunk(factors, q), chunk(fy, q), cy_send.at[q], cy_recv.at[q], y_to)
    rings = [SplitRingGather(net, x, xp, xm, row_slot(zl), factors)]
    own = pltpu.make_async_copy(factors, row_slot(zl)(x), local.at[0])
    own.start()
    load_green.start()
    load_fock.start()
    load_start.start()

    def next_slab(k):
        slab = slabs[k]
        slot = row_slot(slab)(x)
        arrived(slot, z_recv.at[slab])
        up = slab < zl
        where = device(t, x, y, 4 * zh + jnp.where(up, (zl + 1) % 4, (zl + 3) % 4))
        along_z(slot, slab, jnp.where(up, zl < 3, zl > 0), where, 1 + k)
        rings.append(SplitRingGather(net, x, xp, xm, row_slot(slab)))

    def cols_z(q):
        arrived(chunk(fy, q), cy_recv.at[q])
        for h in range(2):
            go(chunk(fy, q), chunk(fz.at[zh], q), cz_send.at[4 * h + q], cz_recv.at[4 * zh + q], z_to[h])

    def cols_x(q):
        e = source_z % 2
        for h in range(2):
            arrived(chunk(fz.at[h], q), cz_recv.at[4 * h + q])
            go(chunk(fz.at[h], q), col_slot(e, x, q), cx_send.at[4 * h + q], cx_recv.at[4 * e + q], x_to[h])

    col_up, col_down, far_cols = {}, {}, []

    def cols_y(q):
        for e in range(2):
            mine = col_slot(e, entry_x(y, e), q)
            arrived(mine, cx_recv.at[4 * e + q])
            col_up[e, q] = net.put(mine, mine, yp)
            col_down[e, q] = net.put(mine, mine, ym)

    def cols_forward(q):
        for e in range(2):
            first, neighbour, where = (col_down[e, q], (y + 1) % 4, ym) if q % 2 else (col_up[e, q], (y + 3) % 4, yp)
            first.wait_recv()
            passed = col_slot(e, entry_x(neighbour, e), q)
            far_cols.append(net.put(passed, passed, where))

    for q in range(4):
        cols_z(q)
    rings[0].forward()
    next_slab(1)
    cols_x(0)
    cols_x(1)
    cols_y(0)
    cols_x(2)
    cols_y(1)
    cols_x(3)
    rings[1].forward()
    next_slab(2)
    cols_y(2)
    cols_forward(0)
    cols_y(3)
    cols_forward(1)
    next_slab(3)
    rings[2].forward()
    cols_forward(2)
    cols_forward(3)
    rings[3].forward()
    load_start.wait()
    for p in range(PARTS):
        x0[p] = x0f[:, W * p : W * (p + 1)].astype(BF16)
    for e in range(2):
        for q in range(4):
            (col_up if q % 2 else col_down)[e, q].wait_recv()
    for copy in far_cols:
        copy.wait_recv()

    load_green.wait()
    load_fock.wait()
    own.wait()

    def sig_copy(u):
        return pltpu.make_async_remote_copy(
            src_ref=sgs.at[u], dst_ref=sgr.at[u], send_sem=sig_send.at[u], recv_sem=sig_recv.at[u],
            device_id=other, device_id_type=pl.DeviceIdType.MESH,
        )

    def slab_sigma(slab):
        row0 = pl.multiple_of(SLAB * slab, 128)

        @pl.loop(0, BLOCK // TILE)
        def _(j):
            col0 = pl.multiple_of(TILE * j, TILE)
            total = jnp.zeros((SLAB, TILE), F32)
            for p in range(2):
                product = lax.dot_general(
                    frow[p, pl.ds(row0, SLAB), :], fcol[p, pl.ds(col0, TILE), :], NT, preferred_element_type=F32
                )
                total = total + product * grn[p, pl.ds(row0, SLAB), pl.ds(col0, TILE)].astype(F32)
            bands = []
            for b in range(SLAB // 128):
                keep = mask[6 * r + (3 * slab + b) // 2, 3 * c + j].astype(F32)
                bands.append(total[128 * b : 128 * (b + 1)] * keep)
            kept = jnp.concatenate(bands, axis=0)

            @pl.when(slab // 2 == t)
            def _():
                sig[slab % 2, :, pl.ds(col0, TILE)] = kept

            @pl.when(slab // 2 != t)
            def _():
                sgs[slab % 2, :, pl.ds(col0, TILE)] = kept.astype(BF16)

        @pl.when(slab // 2 != t)
        def _():
            sig_copy(slab % 2).start()

    center = 0.5 * (upper[0] + lower[0])
    half_width = 0.5 * (upper[0] - lower[0])

    def make_operator(which):
        for slab in which:
            u = slab % 2
            sig_copy(u).wait_recv()
            rows = pl.ds(pl.multiple_of(SLAB * u, 128), SLAB)
            shifted = fck[rows, :].astype(F32) + (sig[u] + sgr[u].astype(F32))
            row_ids = lax.broadcasted_iota(jnp.int32, (SLAB, BLOCK), 0) + (2 * BLOCK * r + SLAB * slab)
            col_ids = lax.broadcasted_iota(jnp.int32, (SLAB, BLOCK), 1) + BLOCK * c
            shifted = jnp.where(row_ids == col_ids, shifted - center, shifted)
            op[rows, :] = (shifted / half_width).astype(BF16)

    rings[0].finish()
    slab_sigma(slabs[0])
    rings[1].finish()
    slab_sigma(slabs[1])
    pl.when(zl // 2 == t)(lambda: make_operator(slabs[:2]))
    rings[2].finish()
    slab_sigma(slabs[2])
    rings[3].finish()
    slab_sigma(slabs[3])
    pl.when(zl // 2 != t)(lambda: make_operator(slabs[2:]))

    def direct_reduce(me, plus, minus, opposite, size, ready, part, stage, near, far):
        def rows(i):
            return pl.ds(pl.multiple_of(size * i, 32), size)

        copies = []
        for k, where, into in ((2, opposite, far), (1, plus, near.at[0]), (3, minus, near.at[1])):
            at = rows((me + k) % 4)
            ready((me + k) % 4)
            stage[at, :] = part[at, :].astype(BF16)
            copies.append(net.put(stage.at[at, :], into, where))
        ready(me)
        yield
        for copy in copies:
            copy.wait_recv()
        at = rows(me)
        part[at, :] = part[at, :] + far[...].astype(F32) + (near[0].astype(F32) + near[1].astype(F32))

    def ring_reduce(me, plus, minus, size, ready, part, stage, near, far):
        h = size // 2

        def rows(i, half):
            return pl.ds(pl.multiple_of(size * i + h * half, 16), h)

        def push(i, half, there, where):
            return net.put(stage.at[rows(i, half), :], there, where)

        a, b, opposite = (me + 1) % 4, (me + 3) % 4, (me + 2) % 4
        ready(opposite)
        for half in range(2):
            stage[rows(opposite, half), :] = part[rows(opposite, half), :].astype(BF16)
        far_up = push(opposite, 0, far.at[0], plus)
        far_down = push(opposite, 1, far.at[1], minus)
        ready(a)
        stage[rows(a, 1), :] = part[rows(a, 1), :].astype(BF16)
        up1 = push(a, 1, near.at[1], plus)
        ready(b)
        stage[rows(b, 0), :] = part[rows(b, 0), :].astype(BF16)
        down0 = push(b, 0, near.at[2], minus)
        ready(me)
        yield
        far_up.wait_recv()
        stage[rows(a, 0), :] = (part[rows(a, 0), :] + far[0].astype(F32)).astype(BF16)
        up0 = push(a, 0, near.at[0], plus)
        far_down.wait_recv()
        stage[rows(b, 1), :] = (part[rows(b, 1), :] + far[1].astype(F32)).astype(BF16)
        down1 = push(b, 1, near.at[3], minus)
        yield
        for copy in (up1, down0, up0, down1):
            copy.wait_recv()
        for half in range(2):
            at = rows(me, half)
            part[at, :] = part[at, :] + near[half].astype(F32) + near[2 + half].astype(F32)

    def across(block, n, p):
        prt = part.at[p]

        def ready(i):
            at = pl.ds(pl.multiple_of(QUARTER * i, 64), QUARTER)
            prt[at, :] = jnp.dot(op[at, :], block[...], preferred_element_type=F32)

        k = PARTS * n + p
        yield from ring_reduce(x, xp, xm, QUARTER, ready, prt, stage.at[k], near.at[k], far.at[k])
        zout[k] = prt[pl.ds(pl.multiple_of(QUARTER * x, 64), QUARTER), :].astype(BF16)

        def share(s):
            return pl.ds(pl.multiple_of(SHARE * s, 16), SHARE)

        copies = [net.put(zout.at[k, share(zls[d]), :], zin.at[k, d - 1], zdev[d]) for d in (1, 2, 3)]
        yield
        total = prt[pl.ds(pl.multiple_of(QUARTER * x + SHARE * zl, 16), SHARE), :]
        for d in (1, 2, 3):
            copies[d - 1].wait_recv()
            total = total + zin[k, d - 1].astype(F32)
        return total

    def gather_rows(buffer):
        def slots(s):
            def slot(i, half=None):
                rows = pl.ds(pl.multiple_of(QUARTER * i + SHARE * s, 16), SHARE)
                return buffer.at[rows, :] if half is None else buffer.at[rows, pl.ds(W // 2 * half, W // 2)]
            return slot

        here = slots(zl)(x)
        zc = [net.put(here, here, zdev[d]) for d in (1, 2, 3)]
        rings = [RingGather(net, x, xp, xm, slots(zl))]
        yield
        for d in (1, 2, 3):
            zc[d - 1].wait_recv()
            rings.append(RingGather(net, x, xp, xm, slots(zls[d])))
        yield
        for ring in rings:
            ring.forward()
        yield
        for ring in rings:
            ring.finish()

    far_half = pl.ds(pl.multiple_of(SLAB * (1 - t), SLAB), SLAB)
    near_half = pl.ds(pl.multiple_of(SLAB * t, SLAB), SLAB)
    rows_o = pl.ds(pl.multiple_of(BLOCK * (1 - t), BLOCK), BLOCK)
    my_share = pl.ds(pl.multiple_of(QUARTER * x + SHARE * zl, 16), SHARE)
    my_out = pl.ds(pl.multiple_of(BLOCK * t + QUARTER * x + SHARE * zl, 16), SHARE)
    shard = SLAB // 4
    my_shard = pl.ds(pl.multiple_of(shard * y, 32), shard)
    mine2 = pl.ds(pl.multiple_of(SLAB * t + shard * y, 32), shard)
    stores = []

    def transpose():
        yield
        for i in range(3):
            for j in range(3):
                opt[pl.ds(TILE * j, TILE), pl.ds(TILE * i, TILE)] = op[pl.ds(TILE * i, TILE), pl.ds(TILE * j, TILE)].T

    def steps(p):
        cols = pl.ds(W * p, W)
        total = yield from across(x0.at[p], 0, p)
        y1own[p] = total
        y1[p, my_share, :] = total.astype(BF16)
        yield from gather_rows(y1.at[p])

        cstage[p] = jnp.dot(opt[far_half, :], y1[p], preferred_element_type=F32).astype(BF16)
        swap = net.put(cstage.at[p], cin.at[p], other)
        part2[p] = jnp.dot(opt[near_half, :], y1[p], preferred_element_type=F32)
        swap.wait_recv()
        part2[p] = part2[p] + cin[p].astype(F32)
        yield from direct_reduce(
            y, yp, ym, yo, shard, lambda i: None, part2.at[p], stage2.at[p], near2.at[p], far2.at[p]
        )
        hout[p] = part2[p, my_shard, :].astype(BF16)
        over = net.put(hout.at[p], hin.at[p], hdev)
        yield
        over.wait_recv()
        total = part2[p, my_shard, :] + hin[p].astype(F32)

        def slot2(i, half=None):
            rows = pl.ds(pl.multiple_of(SLAB * t + shard * i, 32), shard)
            return y2.at[p, rows, :] if half is None else y2.at[p, rows, pl.ds(W // 2 * half, W // 2)]

        y2[p, mine2, :] = (2.0 * total - x0f[mine2, cols]).astype(BF16)
        ring = DirectGather(net, y, yp, ym, yo, slot2)
        yield
        ring.finish()
        both = net.put(y2.at[p, near_half, :], y2.at[p, near_half, :], other)
        yield
        both.wait_recv()

        total = yield from across(y2.at[p], 1, p)
        y3[p, my_out, :] = (2.0 * total - y1own[p]).astype(BF16)
        yield from gather_rows(y3.at[p, rows_t, :])
        last = net.put(y3.at[p, rows_t, :], y3.at[p, rows_t, :], other)
        stores.append(pltpu.make_async_copy(y3.at[p, rows_t, :], out.at[rows_t, cols], local.at[4 + 2 * p]))
        stores[-1].start()
        yield
        last.wait_recv()
        stores.append(pltpu.make_async_copy(y3.at[p, rows_o, :], out.at[rows_o, cols], local.at[5 + 2 * p]))
        stores[-1].start()

    in_turn(*[steps(p) for p in range(PARTS)], transpose())

    for copy in sends:
        copy.wait_send()
    for condition, copy in z_sent:
        pl.when(condition)(lambda: copy.wait_send())
    for u in range(2):
        sig_copy(u).wait_send()
    net.drain()
    for copy in stores:
        copy.wait()


def on_device(fock, green, factors, tile_mask, start_block, lower_edge, upper_edge):
    anywhere, smem = pl.BlockSpec(memory_space=pl.ANY), pl.BlockSpec(memory_space=pltpu.SMEM)
    v, dma = pltpu.VMEM, pltpu.SemaphoreType.DMA
    q2, s2 = QUARTER // 2, SLAB // 8
    result = pl.pallas_call(
        kernel,
        out_shape=jax.ShapeDtypeStruct((2 * BLOCK, SUB), BF16),
        in_specs=[anywhere] * 4 + [smem] * 3,
        out_specs=anywhere,
        scratch_shapes=[
            v((2, 2 * BLOCK, 768), BF16),
            v((2, BLOCK, 768), BF16),
            v((2, PIECE, 768), BF16),
            v((2, 2, PIECE, 768), BF16),
            v((2, 2 * BLOCK, BLOCK), BF16),
            v((BLOCK, BLOCK), BF16),
            v((BLOCK, SUB), F32),
            v((PARTS, BLOCK, W), BF16),
            v((2, SLAB, BLOCK), F32),
            v((2, SLAB, BLOCK), BF16),
            v((2, SLAB, BLOCK), BF16),
            v((BLOCK, BLOCK), BF16),
            v((BLOCK, BLOCK), BF16),
            v((PARTS, BLOCK, W), F32),
            v((2 * PARTS, BLOCK, W), BF16),
            v((2 * PARTS, 4, q2, W), BF16),
            v((2 * PARTS, 2, q2, W), BF16),
            v((2 * PARTS, 3, SHARE, W), BF16),
            v((2 * PARTS, QUARTER, W), BF16),
            v((PARTS, BLOCK, W), BF16),
            v((PARTS, SHARE, W), F32),
            v((PARTS, SLAB, W), F32),
            v((PARTS, SLAB, W), BF16),
            v((PARTS, SLAB, W), BF16),
            v((PARTS, SLAB, W), BF16),
            v((PARTS, 2, 2 * s2, W), BF16),
            v((PARTS, 2 * s2, W), BF16),
            v((PARTS, 2 * s2, W), BF16),
            v((PARTS, 2 * s2, W), BF16),
            v((PARTS, BLOCK, W), BF16),
            v((PARTS, 2 * BLOCK, W), BF16),
            dma((COPIES,)),
            dma((COPIES,)),
            dma((5,)),
            dma((4,)),
            dma((4,)),
            dma((4,)),
            dma((8,)),
            dma((8,)),
            dma((8,)),
            dma((8,)),
            dma((2,)),
            dma((2,)),
            dma((4 + 2 * PARTS,)),
        ],
        compiler_params=pltpu.CompilerParams(
            collective_id=0, has_side_effects=True, vmem_limit_bytes=52 * 2**20
        ),
        name="filter_kernel",
    )(factors, green, fock, start_block, tile_mask, lower_edge, upper_edge)
    return result.astype(F32)


def solution(mesh):
    placed = (
        P("row", "col"),
        P("tau", "row", "col"),
        P("tau", ("row", "col"), None),
        P(),
        P("col", None),
        P(),
        P(),
    )
    return jax.shard_map(
        on_device, mesh=mesh, in_specs=placed, out_specs=P("row", None), check_vma=False
    )
```

```python
import jax
import jax.numpy as jnp
from jax import lax
from jax.experimental import pallas as pl
from jax.experimental.pallas import tpu as pltpu
from jax.sharding import PartitionSpec as P

F32, BF16 = jnp.float32, jnp.bfloat16
NT = (((1,), (1,)), ((), ()))

PIECE = 96
CHUNK = PIECE // 2
SLAB = 384
BLOCK = 768
SUB = 512
PARTS = 2
W = SUB // PARTS
COPIES = 48 + 72 * PARTS
TILE = 256
QUARTER = BLOCK // 4
SHARE = QUARTER // 4


def device(t, x, y, z):
    return (t, 2 * y + z // 4, 4 * (z % 4) + x)


class Net:
    def __init__(self, send, recv):
        self.send, self.recv, self.count, self.started = send, recv, 0, []

    def put(self, src, dst, where):
        i = self.count
        self.count += 1
        copy = pltpu.make_async_remote_copy(
            src_ref=src, dst_ref=dst, send_sem=self.send.at[i], recv_sem=self.recv.at[i],
            device_id=where, device_id_type=pl.DeviceIdType.MESH,
        )
        copy.start()
        self.started.append(copy)
        return copy

    def drain(self):
        assert self.count == COPIES
        for copy in self.started:
            copy.wait_send()


class RingGather:
    def __init__(self, net, me, plus, minus, slot, source=None):
        self.net, self.me, self.plus, self.minus, self.slot = net, me, plus, minus, slot
        source = slot(me) if source is None else source
        self.up = net.put(source, slot(me), plus)
        self.down = net.put(source, slot(me), minus)

    def forward(self):
        before, after = (self.me + 3) % 4, (self.me + 1) % 4
        self.up.wait_recv()
        self.up2 = self.net.put(self.slot(before, 0), self.slot(before, 0), self.plus)
        self.down.wait_recv()
        self.down2 = self.net.put(self.slot(after, 1), self.slot(after, 1), self.minus)

    def finish(self):
        self.up2.wait_recv()
        self.down2.wait_recv()


class SplitRingGather(RingGather):
    def __init__(self, net, me, plus, minus, slot, source=None):
        self.net, self.me, self.plus, self.minus, self.slot = net, me, plus, minus, slot

        def half(h, where):
            src = slot(me, h) if source is None else source.at[h]
            return net.put(src, slot(me, h), where)

        self.up, self.down = half(0, plus), half(1, minus)
        self.rest = [half(1, plus), half(0, minus)]

    def finish(self):
        for copy in self.rest:
            copy.wait_recv()
        super().finish()


class DirectGather:
    def __init__(self, net, me, plus, minus, opposite, slot):
        mine = slot(me)
        self.copies = [net.put(mine, mine, where) for where in (opposite, plus, minus)]


class Send:
    def __init__(self, src, dst, send_sem, recv_sem, where, is_self):
        self.is_self = is_self
        self.remote = pltpu.make_async_remote_copy(
            src_ref=src, dst_ref=dst, send_sem=send_sem, recv_sem=recv_sem,
            device_id=where, device_id_type=pl.DeviceIdType.MESH,
        )
        self.local = pltpu.make_async_copy(src, dst, recv_sem)

    def start(self):
        pl.when(self.is_self)(lambda: self.local.start())
        pl.when(jnp.logical_not(self.is_self))(lambda: self.remote.start())

    def wait_send(self):
        pl.when(jnp.logical_not(self.is_self))(lambda: self.remote.wait_send())


def in_turn(*tasks):
    tasks = list(tasks)
    while tasks:
        for task in list(tasks):
            try:
                next(task)
            except StopIteration:
                tasks.remove(task)


def kernel(
    factors, green, fock, start, mask, lower, upper, out,
    frow, fcol, fy, fz, grn, fck, x0f, x0, sig, sgs, sgr, op, opt, part, stage, near, far, zin, zout,
    y1, y1own, part2, cstage, cin, stage2, near2, far2, hout, hin, y2, y3,
    send, recv, z_send, z_recv, cy_send, cy_recv, cz_send, cz_recv, cx_send, cx_recv, sig_send, sig_recv, local,
):
    t, r, c = lax.axis_index("tau"), lax.axis_index("row"), lax.axis_index("col")
    x, y, zl, zh = c % 4, r // 2, c // 4, r % 2
    z = 4 * zh + zl
    xp, xm = device(t, (x + 1) % 4, y, z), device(t, (x + 3) % 4, y, z)
    yp, ym = device(t, x, (y + 1) % 4, z), device(t, x, (y + 3) % 4, z)
    yo = device(t, x, (y + 2) % 4, z)
    zls = (zl, zl + 1 - 2 * (zl % 2), (zl + 2) % 4, 3 - zl)
    zdev = [device(t, x, y, 4 * zh + s) for s in zls]
    hdev = device(t, x, y, 4 * (1 - zh) + zl)
    other = device(1 - t, x, y, z)

    def by_zl(*values):
        return jnp.where(zl == 0, values[0], jnp.where(zl == 1, values[1], jnp.where(zl == 2, values[2], values[3])))

    slabs = (zl, by_zl(1, 0, 3, 2), by_zl(2, 2, 1, 1), by_zl(3, 3, 0, 0))

    entry = (x + y + z) % 4
    home_y = (y - x - z + 12) % 4
    source_z = (y - x - zl + 8) % 4
    to_x = [source_z // 2 + 2 * h for h in range(2)]

    def entry_x(at_y, e):
        return (at_y - zl - 2 * x - e + 12) % 4

    def along(i, j, k):
        return device(t, i, j, k), (i == x) & (j == y) & (k == z)

    y_to, y_from = along(x, entry, z), along(x, home_y, z)
    z_to = [along(x, y, home_y + 4 * h) for h in range(2)]
    z_from = [along(x, y, source_z + 4 * h) for h in range(2)]
    x_to = [along(to_x[h], y, z) for h in range(2)]
    x_from = [along(entry_x(y, e), y, z) for e in range(2)]

    rows_t = pl.ds(pl.multiple_of(BLOCK * t, BLOCK), BLOCK)
    load_green = pltpu.make_async_copy(green, grn, local.at[1])
    load_fock = pltpu.make_async_copy(fock.at[rows_t, :], fck, local.at[2])
    load_start = pltpu.make_async_copy(start, x0f, local.at[3])

    barrier = pltpu.get_barrier_semaphore()
    greeted = [xp, xm, yp, ym, yo, *zdev[1:], hdev, other]
    greeted += [where for where, _ in [y_to, y_from] + z_to + z_from + x_to + x_from]
    for where in greeted:
        pl.semaphore_signal(barrier, inc=1, device_id=where, device_id_type=pl.DeviceIdType.MESH)
    pl.semaphore_wait(barrier, len(greeted))

    net = Net(send, recv)

    def row_slot(slab):
        def slot(i, half=None):
            rows = pl.ds(pl.multiple_of(SLAB * slab + PIECE * i, 32), PIECE)
            return frow.at[:, rows, :] if half is None else frow.at[half, rows, :]
        return slot

    def chunk(ref, q, first=0):
        return ref.at[q // 2, pl.ds(pl.multiple_of(first + CHUNK * (q % 2), 16), CHUNK), :]

    def col_slot(e, from_x, q):
        return chunk(fcol, q, PIECE * (4 * e + from_x))

    sends = []

    def go(src, dst, send_sem, recv_sem, target):
        copy = Send(src, dst, send_sem, recv_sem, *target)
        copy.start()
        sends.append(copy)

    def arrived(dst, recv_sem):
        pltpu.make_async_copy(dst, dst, recv_sem).wait()

    def along_z(source, slab, condition, where, i):
        copy = pltpu.make_async_remote_copy(
            src_ref=source, dst_ref=row_slot(slab)(x), send_sem=z_send.at[i], recv_sem=z_recv.at[slab],
            device_id=where, device_id_type=pl.DeviceIdType.MESH,
        )
        pl.when(condition)(lambda: copy.start())
        z_sent.append((condition, copy))

    z_sent = []
    z_up, z_down = device(t, x, y, 4 * zh + (zl + 1) % 4), device(t, x, y, 4 * zh + (zl + 3) % 4)
    along_z(factors, zl, zl < 3, z_up, 0)
    along_z(factors, zl, zl > 0, z_down, 1)
    for q in range(4):
        go(chunk(factors, q), chunk(fy, q), cy_send.at[q], cy_recv.at[q], y_to)
    rings = [SplitRingGather(net, x, xp, xm, row_slot(zl), factors)]
    own = pltpu.make_async_copy(factors, row_slot(zl)(x), local.at[0])
    own.start()
    load_green.start()
    load_fock.start()
    load_start.start()

    def next_slab(k):
        slab = slabs[k]
        slot = row_slot(slab)(x)
        arrived(slot, z_recv.at[slab])
        up = slab < zl
        where = device(t, x, y, 4 * zh + jnp.where(up, (zl + 1) % 4, (zl + 3) % 4))
        along_z(slot, slab, jnp.where(up, zl < 3, zl > 0), where, 1 + k)
        rings.append(SplitRingGather(net, x, xp, xm, row_slot(slab)))

    def cols_z(q):
        arrived(chunk(fy, q), cy_recv.at[q])
        for h in range(2):
            go(chunk(fy, q), chunk(fz.at[zh], q), cz_send.at[4 * h + q], cz_recv.at[4 * zh + q], z_to[h])

    def cols_x(q):
        e = source_z % 2
        for h in range(2):
            arrived(chunk(fz.at[h], q), cz_recv.at[4 * h + q])
            go(chunk(fz.at[h], q), col_slot(e, x, q), cx_send.at[4 * h + q], cx_recv.at[4 * e + q], x_to[h])

    col_up, col_down, far_cols = {}, {}, []

    def cols_y(q):
        for e in range(2):
            mine = col_slot(e, entry_x(y, e), q)
            arrived(mine, cx_recv.at[4 * e + q])
            col_up[e, q] = net.put(mine, mine, yp)
            col_down[e, q] = net.put(mine, mine, ym)

    def cols_forward(q):
        for e in range(2):
            first, neighbour, where = (col_down[e, q], (y + 1) % 4, ym) if q % 2 else (col_up[e, q], (y + 3) % 4, yp)
            first.wait_recv()
            passed = col_slot(e, entry_x(neighbour, e), q)
            far_cols.append(net.put(passed, passed, where))

    for q in range(4):
        cols_z(q)
    rings[0].forward()
    next_slab(1)
    cols_x(0)
    cols_x(1)
    cols_y(0)
    cols_x(2)
    cols_y(1)
    cols_x(3)
    rings[1].forward()
    next_slab(2)
    cols_y(2)
    cols_forward(0)
    cols_y(3)
    cols_forward(1)
    next_slab(3)
    rings[2].forward()
    cols_forward(2)
    cols_forward(3)
    rings[3].forward()
    load_start.wait()
    for p in range(PARTS):
        x0[p] = x0f[:, W * p : W * (p + 1)].astype(BF16)
    for e in range(2):
        for q in range(4):
            (col_up if q % 2 else col_down)[e, q].wait_recv()
    for copy in far_cols:
        copy.wait_recv()

    load_green.wait()
    load_fock.wait()
    own.wait()

    def sig_copy(u):
        return pltpu.make_async_remote_copy(
            src_ref=sgs.at[u], dst_ref=sgr.at[u], send_sem=sig_send.at[u], recv_sem=sig_recv.at[u],
            device_id=other, device_id_type=pl.DeviceIdType.MESH,
        )

    def slab_sigma(slab):
        row0 = pl.multiple_of(SLAB * slab, 128)

        @pl.loop(0, BLOCK // TILE)
        def _(j):
            col0 = pl.multiple_of(TILE * j, TILE)
            total = jnp.zeros((SLAB, TILE), F32)
            for p in range(2):
                product = lax.dot_general(
                    frow[p, pl.ds(row0, SLAB), :], fcol[p, pl.ds(col0, TILE), :], NT, preferred_element_type=F32
                )
                total = total + product * grn[p, pl.ds(row0, SLAB), pl.ds(col0, TILE)].astype(F32)
            bands = []
            for b in range(SLAB // 128):
                keep = mask[6 * r + (3 * slab + b) // 2, 3 * c + j].astype(F32)
                bands.append(total[128 * b : 128 * (b + 1)] * keep)
            kept = jnp.concatenate(bands, axis=0)

            @pl.when(slab // 2 == t)
            def _():
                sig[slab % 2, :, pl.ds(col0, TILE)] = kept

            @pl.when(slab // 2 != t)
            def _():
                sgs[slab % 2, :, pl.ds(col0, TILE)] = kept.astype(BF16)

        @pl.when(slab // 2 != t)
        def _():
            sig_copy(slab % 2).start()

    center = 0.5 * (upper[0] + lower[0])
    half_width = 0.5 * (upper[0] - lower[0])

    def make_operator(which):
        for slab in which:
            u = slab % 2
            sig_copy(u).wait_recv()
            rows = pl.ds(pl.multiple_of(SLAB * u, 128), SLAB)
            shifted = fck[rows, :].astype(F32) + (sig[u] + sgr[u].astype(F32))
            row_ids = lax.broadcasted_iota(jnp.int32, (SLAB, BLOCK), 0) + (2 * BLOCK * r + SLAB * slab)
            col_ids = lax.broadcasted_iota(jnp.int32, (SLAB, BLOCK), 1) + BLOCK * c
            shifted = jnp.where(row_ids == col_ids, shifted - center, shifted)
            op[rows, :] = (shifted / half_width).astype(BF16)

    rings[0].finish()
    slab_sigma(slabs[0])
    rings[1].finish()
    slab_sigma(slabs[1])
    pl.when(zl // 2 == t)(lambda: make_operator(slabs[:2]))
    rings[2].finish()
    slab_sigma(slabs[2])
    rings[3].finish()
    slab_sigma(slabs[3])
    pl.when(zl // 2 != t)(lambda: make_operator(slabs[2:]))

    def direct_reduce(me, plus, minus, opposite, size, ready, part, stage, near, far):
        def rows(i):
            return pl.ds(pl.multiple_of(size * i, 32), size)

        copies = []
        for k, where, into in ((2, opposite, far), (1, plus, near.at[0]), (3, minus, near.at[1])):
            at = rows((me + k) % 4)
            ready((me + k) % 4)
            stage[at, :] = part[at, :].astype(BF16)
            copies.append(net.put(stage.at[at, :], into, where))
        ready(me)
        yield
        for copy in copies:
            copy.wait_recv()
        at = rows(me)
        part[at, :] = part[at, :] + far[...].astype(F32) + (near[0].astype(F32) + near[1].astype(F32))

    def ring_reduce(me, plus, minus, size, ready, part, stage, near, far):
        h = size // 2

        def rows(i, half):
            return pl.ds(pl.multiple_of(size * i + h * half, 16), h)

        def push(i, half, there, where):
            return net.put(stage.at[rows(i, half), :], there, where)

        a, b, opposite = (me + 1) % 4, (me + 3) % 4, (me + 2) % 4
        ready(opposite)
        for half in range(2):
            stage[rows(opposite, half), :] = part[rows(opposite, half), :].astype(BF16)
        far_up = push(opposite, 0, far.at[0], plus)
        far_down = push(opposite, 1, far.at[1], minus)
        ready(a)
        stage[rows(a, 1), :] = part[rows(a, 1), :].astype(BF16)
        up1 = push(a, 1, near.at[1], plus)
        ready(b)
        stage[rows(b, 0), :] = part[rows(b, 0), :].astype(BF16)
        down0 = push(b, 0, near.at[2], minus)
        ready(me)
        yield
        far_up.wait_recv()
        stage[rows(a, 0), :] = (part[rows(a, 0), :] + far[0].astype(F32)).astype(BF16)
        up0 = push(a, 0, near.at[0], plus)
        far_down.wait_recv()
        stage[rows(b, 1), :] = (part[rows(b, 1), :] + far[1].astype(F32)).astype(BF16)
        down1 = push(b, 1, near.at[3], minus)
        yield
        for copy in (up1, down0, up0, down1):
            copy.wait_recv()
        for half in range(2):
            at = rows(me, half)
            part[at, :] = part[at, :] + near[half].astype(F32) + near[2 + half].astype(F32)

    def across(block, n, p):
        prt = part.at[p]

        def ready(i):
            at = pl.ds(pl.multiple_of(QUARTER * i, 64), QUARTER)
            prt[at, :] = jnp.dot(op[at, :], block[...], preferred_element_type=F32)

        k = PARTS * n + p
        yield from ring_reduce(x, xp, xm, QUARTER, ready, prt, stage.at[k], near.at[k], far.at[k])
        zout[k] = prt[pl.ds(pl.multiple_of(QUARTER * x, 64), QUARTER), :].astype(BF16)

        def share(s):
            return pl.ds(pl.multiple_of(SHARE * s, 16), SHARE)

        copies = [net.put(zout.at[k, share(zls[d]), :], zin.at[k, d - 1], zdev[d]) for d in (1, 2, 3)]
        yield
        total = prt[pl.ds(pl.multiple_of(QUARTER * x + SHARE * zl, 16), SHARE), :]
        for d in (1, 2, 3):
            copies[d - 1].wait_recv()
            total = total + zin[k, d - 1].astype(F32)
        return total

    def gather_rows(buffer, complete=lambda i: None):
        def slots(s):
            def slot(i, half=None):
                rows = pl.ds(pl.multiple_of(QUARTER * i + SHARE * s, 16), SHARE)
                return buffer.at[rows, :] if half is None else buffer.at[rows, pl.ds(W // 2 * half, W // 2)]
            return slot

        here = slots(zl)(x)
        zc = [net.put(here, here, zdev[d]) for d in (1, 2, 3)]
        rings = [RingGather(net, x, xp, xm, slots(zl))]
        yield
        for d in (1, 2, 3):
            zc[d - 1].wait_recv()
            rings.append(RingGather(net, x, xp, xm, slots(zls[d])))
        complete(x)
        yield
        for ring in rings:
            ring.forward()
        complete((x + 3) % 4)
        complete((x + 1) % 4)
        yield
        for ring in rings:
            ring.finish()
        complete((x + 2) % 4)

    far_half = pl.ds(pl.multiple_of(SLAB * (1 - t), SLAB), SLAB)
    near_half = pl.ds(pl.multiple_of(SLAB * t, SLAB), SLAB)
    rows_o = pl.ds(pl.multiple_of(BLOCK * (1 - t), BLOCK), BLOCK)
    my_share = pl.ds(pl.multiple_of(QUARTER * x + SHARE * zl, 16), SHARE)
    my_out = pl.ds(pl.multiple_of(BLOCK * t + QUARTER * x + SHARE * zl, 16), SHARE)
    shard = SLAB // 4
    my_shard = pl.ds(pl.multiple_of(shard * y, 32), shard)
    mine2 = pl.ds(pl.multiple_of(SLAB * t + shard * y, 32), shard)
    stores = []

    def transpose():
        yield
        for i in range(3):
            for j in range(3):
                opt[pl.ds(TILE * j, TILE), pl.ds(TILE * i, TILE)] = op[pl.ds(TILE * i, TILE), pl.ds(TILE * j, TILE)].T

    def steps(p):
        cols = pl.ds(W * p, W)
        total = yield from across(x0.at[p], 0, p)
        y1own[p] = total
        y1[p, my_share, :] = total.astype(BF16)
        yield from gather_rows(y1.at[p])

        cstage[p] = jnp.dot(opt[far_half, :], y1[p], preferred_element_type=F32).astype(BF16)
        swap = net.put(cstage.at[p], cin.at[p], other)
        part2[p] = jnp.dot(opt[near_half, :], y1[p], preferred_element_type=F32)
        swap.wait_recv()
        part2[p] = part2[p] + cin[p].astype(F32)
        yield from direct_reduce(
            y, yp, ym, yo, shard, lambda i: None, part2.at[p], stage2.at[p], near2.at[p], far2.at[p]
        )
        hout[p] = part2[p, my_shard, :].astype(BF16)
        over = net.put(hout.at[p], hin.at[p], hdev)
        yield
        over.wait_recv()
        total = part2[p, my_shard, :] + hin[p].astype(F32)

        def slot2(i, half=None):
            rows = pl.ds(pl.multiple_of(SLAB * t + shard * i, 32), shard)
            return y2.at[p, rows, :] if half is None else y2.at[p, rows, pl.ds(W // 2 * half, W // 2)]

        y2[p, mine2, :] = (2.0 * total - x0f[mine2, cols]).astype(BF16)
        ring = DirectGather(net, y, yp, ym, yo, slot2)
        yield
        both = [net.put(slot2(y), slot2(y), other)]
        for copy, i in zip(ring.copies[1:] + ring.copies[:1], (y + 3, y + 1, y + 2)):
            copy.wait_recv()
            both.append(net.put(slot2(i % 4), slot2(i % 4), other))
        yield
        for copy in both:
            copy.wait_recv()

        total = yield from across(y2.at[p], 1, p)
        y3[p, my_out, :] = (2.0 * total - y1own[p]).astype(BF16)
        last = []

        def pass_on(i):
            quarter = y3.at[p, pl.ds(pl.multiple_of(BLOCK * t + QUARTER * i, 64), QUARTER), :]
            last.append(net.put(quarter, quarter, other))

        yield from gather_rows(y3.at[p, rows_t, :], pass_on)
        stores.append(pltpu.make_async_copy(y3.at[p, rows_t, :], out.at[rows_t, cols], local.at[4 + 2 * p]))
        stores[-1].start()
        yield
        for copy in last:
            copy.wait_recv()
        stores.append(pltpu.make_async_copy(y3.at[p, rows_o, :], out.at[rows_o, cols], local.at[5 + 2 * p]))
        stores[-1].start()

    in_turn(*[steps(p) for p in range(PARTS)], transpose())

    for copy in sends:
        copy.wait_send()
    for condition, copy in z_sent:
        pl.when(condition)(lambda: copy.wait_send())
    for u in range(2):
        sig_copy(u).wait_send()
    net.drain()
    for copy in stores:
        copy.wait()


def on_device(fock, green, factors, tile_mask, start_block, lower_edge, upper_edge):
    anywhere, smem = pl.BlockSpec(memory_space=pl.ANY), pl.BlockSpec(memory_space=pltpu.SMEM)
    v, dma = pltpu.VMEM, pltpu.SemaphoreType.DMA
    q2, s2 = QUARTER // 2, SLAB // 8
    result = pl.pallas_call(
        kernel,
        out_shape=jax.ShapeDtypeStruct((2 * BLOCK, SUB), BF16),
        in_specs=[anywhere] * 4 + [smem] * 3,
        out_specs=anywhere,
        scratch_shapes=[
            v((2, 2 * BLOCK, 768), BF16),
            v((2, BLOCK, 768), BF16),
            v((2, PIECE, 768), BF16),
            v((2, 2, PIECE, 768), BF16),
            v((2, 2 * BLOCK, BLOCK), BF16),
            v((BLOCK, BLOCK), BF16),
            v((BLOCK, SUB), F32),
            v((PARTS, BLOCK, W), BF16),
            v((2, SLAB, BLOCK), F32),
            v((2, SLAB, BLOCK), BF16),
            v((2, SLAB, BLOCK), BF16),
            v((BLOCK, BLOCK), BF16),
            v((BLOCK, BLOCK), BF16),
            v((PARTS, BLOCK, W), F32),
            v((2 * PARTS, BLOCK, W), BF16),
            v((2 * PARTS, 4, q2, W), BF16),
            v((2 * PARTS, 2, q2, W), BF16),
            v((2 * PARTS, 3, SHARE, W), BF16),
            v((2 * PARTS, QUARTER, W), BF16),
            v((PARTS, BLOCK, W), BF16),
            v((PARTS, SHARE, W), F32),
            v((PARTS, SLAB, W), F32),
            v((PARTS, SLAB, W), BF16),
            v((PARTS, SLAB, W), BF16),
            v((PARTS, SLAB, W), BF16),
            v((PARTS, 2, 2 * s2, W), BF16),
            v((PARTS, 2 * s2, W), BF16),
            v((PARTS, 2 * s2, W), BF16),
            v((PARTS, 2 * s2, W), BF16),
            v((PARTS, BLOCK, W), BF16),
            v((PARTS, 2 * BLOCK, W), BF16),
            dma((COPIES,)),
            dma((COPIES,)),
            dma((5,)),
            dma((4,)),
            dma((4,)),
            dma((4,)),
            dma((8,)),
            dma((8,)),
            dma((8,)),
            dma((8,)),
            dma((2,)),
            dma((2,)),
            dma((4 + 2 * PARTS,)),
        ],
        compiler_params=pltpu.CompilerParams(
            collective_id=0, has_side_effects=True, vmem_limit_bytes=52 * 2**20
        ),
        name="filter_kernel",
    )(factors, green, fock, start_block, tile_mask, lower_edge, upper_edge)
    return result.astype(F32)


def solution(mesh):
    placed = (
        P("row", "col"),
        P("tau", "row", "col"),
        P("tau", ("row", "col"), None),
        P(),
        P("col", None),
        P(),
        P(),
    )
    return jax.shard_map(
        on_device, mesh=mesh, in_specs=placed, out_specs=P("row", None), check_vma=False
    )
```

```python
import jax
import jax.numpy as jnp
from jax import lax
from jax.experimental import pallas as pl
from jax.experimental.pallas import tpu as pltpu
from jax.sharding import PartitionSpec as P

F32, BF16 = jnp.float32, jnp.bfloat16
NT = (((1,), (1,)), ((), ()))

PIECE = 96
CHUNK = PIECE // 2
SLAB = 384
BLOCK = 768
SUB = 512
PARTS = 2
W = SUB // PARTS
COPIES = 48 + 72 * PARTS
TILE = 256
QUARTER = BLOCK // 4
SHARE = QUARTER // 4


def device(t, x, y, z):
    return (t, 2 * y + z // 4, 4 * (z % 4) + x)


class Net:
    def __init__(self, send, recv):
        self.send, self.recv, self.count, self.started = send, recv, 0, []

    def put(self, src, dst, where):
        i = self.count
        self.count += 1
        copy = pltpu.make_async_remote_copy(
            src_ref=src, dst_ref=dst, send_sem=self.send.at[i], recv_sem=self.recv.at[i],
            device_id=where, device_id_type=pl.DeviceIdType.MESH,
        )
        copy.start()
        self.started.append(copy)
        return copy

    def drain(self):
        assert self.count == COPIES
        for copy in self.started:
            copy.wait_send()


class RingGather:
    def __init__(self, net, me, plus, minus, slot, source=None):
        self.net, self.me, self.plus, self.minus, self.slot = net, me, plus, minus, slot
        source = slot(me) if source is None else source
        self.up = net.put(source, slot(me), plus)
        self.down = net.put(source, slot(me), minus)

    def forward(self):
        before, after = (self.me + 3) % 4, (self.me + 1) % 4
        self.up.wait_recv()
        self.up2 = self.net.put(self.slot(before, 0), self.slot(before, 0), self.plus)
        self.down.wait_recv()
        self.down2 = self.net.put(self.slot(after, 1), self.slot(after, 1), self.minus)

    def finish(self):
        self.up2.wait_recv()
        self.down2.wait_recv()


class SplitRingGather(RingGather):
    def __init__(self, net, me, plus, minus, slot, source=None):
        self.net, self.me, self.plus, self.minus, self.slot = net, me, plus, minus, slot

        def half(h, where):
            src = slot(me, h) if source is None else source.at[h]
            return net.put(src, slot(me, h), where)

        self.up, self.down = half(0, plus), half(1, minus)
        self.rest = [half(1, plus), half(0, minus)]

    def finish(self):
        for copy in self.rest:
            copy.wait_recv()
        super().finish()


class DirectGather:
    def __init__(self, net, me, plus, minus, opposite, slot):
        mine = slot(me)
        self.copies = [net.put(mine, mine, where) for where in (opposite, plus, minus)]


class Send:
    def __init__(self, src, dst, send_sem, recv_sem, where, is_self):
        self.is_self = is_self
        self.remote = pltpu.make_async_remote_copy(
            src_ref=src, dst_ref=dst, send_sem=send_sem, recv_sem=recv_sem,
            device_id=where, device_id_type=pl.DeviceIdType.MESH,
        )
        self.local = pltpu.make_async_copy(src, dst, recv_sem)

    def start(self):
        pl.when(self.is_self)(lambda: self.local.start())
        pl.when(jnp.logical_not(self.is_self))(lambda: self.remote.start())

    def wait_send(self):
        pl.when(jnp.logical_not(self.is_self))(lambda: self.remote.wait_send())


def in_turn(*tasks):
    tasks = list(tasks)
    while tasks:
        for task in list(tasks):
            try:
                next(task)
            except StopIteration:
                tasks.remove(task)


def kernel(
    factors, green, fock, start, mask, lower, upper, out,
    frow, fcol, fy, fz, grn, fck, x0f, x0, sig, sgs, sgr, op, opt, part, stage, near, far, zin, zout,
    y1, y1own, part2, cstage, cin, stage2, near2, far2, hout, hin, y2, y3,
    send, recv, z_send, z_recv, cy_send, cy_recv, cz_send, cz_recv, cx_send, cx_recv, sig_send, sig_recv, local,
):
    t, r, c = lax.axis_index("tau"), lax.axis_index("row"), lax.axis_index("col")
    x, y, zl, zh = c % 4, r // 2, c // 4, r % 2
    z = 4 * zh + zl
    xp, xm = device(t, (x + 1) % 4, y, z), device(t, (x + 3) % 4, y, z)
    yp, ym = device(t, x, (y + 1) % 4, z), device(t, x, (y + 3) % 4, z)
    yo = device(t, x, (y + 2) % 4, z)
    zls = (zl, zl + 1 - 2 * (zl % 2), (zl + 2) % 4, 3 - zl)
    zdev = [device(t, x, y, 4 * zh + s) for s in zls]
    hdev = device(t, x, y, 4 * (1 - zh) + zl)
    other = device(1 - t, x, y, z)

    def by_zl(*values):
        return jnp.where(zl == 0, values[0], jnp.where(zl == 1, values[1], jnp.where(zl == 2, values[2], values[3])))

    slabs = (zl, by_zl(1, 0, 3, 2), by_zl(2, 2, 1, 1), by_zl(3, 3, 0, 0))

    entry = (x + y + z) % 4
    home_y = (y - x - z + 12) % 4
    source_z = (y - x - zl + 8) % 4
    to_x = [source_z // 2 + 2 * h for h in range(2)]

    def entry_x(at_y, e):
        return (at_y - zl - 2 * x - e + 12) % 4

    def along(i, j, k):
        return device(t, i, j, k), (i == x) & (j == y) & (k == z)

    y_to, y_from = along(x, entry, z), along(x, home_y, z)
    z_to = [along(x, y, home_y + 4 * h) for h in range(2)]
    z_from = [along(x, y, source_z + 4 * h) for h in range(2)]
    x_to = [along(to_x[h], y, z) for h in range(2)]
    x_from = [along(entry_x(y, e), y, z) for e in range(2)]

    rows_t = pl.ds(pl.multiple_of(BLOCK * t, BLOCK), BLOCK)
    load_green = pltpu.make_async_copy(green, grn, local.at[1])
    load_fock = pltpu.make_async_copy(fock.at[rows_t, :], fck, local.at[2])
    load_start = pltpu.make_async_copy(start, x0f, local.at[3])

    barrier = pltpu.get_barrier_semaphore()
    greeted = [xp, xm, yp, ym, yo, *zdev[1:], hdev, other]
    greeted += [where for where, _ in [y_to, y_from] + z_to + z_from + x_to + x_from]
    for where in greeted:
        pl.semaphore_signal(barrier, inc=1, device_id=where, device_id_type=pl.DeviceIdType.MESH)
    pl.semaphore_wait(barrier, len(greeted))

    net = Net(send, recv)

    def row_slot(slab):
        def slot(i, half=None):
            rows = pl.ds(pl.multiple_of(SLAB * slab + PIECE * i, 32), PIECE)
            return frow.at[:, rows, :] if half is None else frow.at[half, rows, :]
        return slot

    def chunk(ref, q, first=0):
        return ref.at[q // 2, pl.ds(pl.multiple_of(first + CHUNK * (q % 2), 16), CHUNK), :]

    def col_slot(e, from_x, q):
        return chunk(fcol, q, PIECE * (4 * e + from_x))

    sends = []

    def go(src, dst, send_sem, recv_sem, target):
        copy = Send(src, dst, send_sem, recv_sem, *target)
        copy.start()
        sends.append(copy)

    def arrived(dst, recv_sem):
        pltpu.make_async_copy(dst, dst, recv_sem).wait()

    def along_z(source, slab, condition, where, i):
        copy = pltpu.make_async_remote_copy(
            src_ref=source, dst_ref=row_slot(slab)(x), send_sem=z_send.at[i], recv_sem=z_recv.at[slab],
            device_id=where, device_id_type=pl.DeviceIdType.MESH,
        )
        pl.when(condition)(lambda: copy.start())
        z_sent.append((condition, copy))

    z_sent = []
    z_up, z_down = device(t, x, y, 4 * zh + (zl + 1) % 4), device(t, x, y, 4 * zh + (zl + 3) % 4)
    along_z(factors, zl, zl < 3, z_up, 0)
    along_z(factors, zl, zl > 0, z_down, 1)
    for q in range(4):
        go(chunk(factors, q), chunk(fy, q), cy_send.at[q], cy_recv.at[q], y_to)
    rings = [SplitRingGather(net, x, xp, xm, row_slot(zl), factors)]
    own = pltpu.make_async_copy(factors, row_slot(zl)(x), local.at[0])
    own.start()
    load_green.start()
    load_fock.start()
    load_start.start()

    def next_slab(k):
        slab = slabs[k]
        slot = row_slot(slab)(x)
        arrived(slot, z_recv.at[slab])
        up = slab < zl
        where = device(t, x, y, 4 * zh + jnp.where(up, (zl + 1) % 4, (zl + 3) % 4))
        along_z(slot, slab, jnp.where(up, zl < 3, zl > 0), where, 1 + k)
        rings.append(SplitRingGather(net, x, xp, xm, row_slot(slab)))

    def cols_z(q):
        arrived(chunk(fy, q), cy_recv.at[q])
        for h in range(2):
            go(chunk(fy, q), chunk(fz.at[zh], q), cz_send.at[4 * h + q], cz_recv.at[4 * zh + q], z_to[h])

    def cols_x(q):
        e = source_z % 2
        for h in range(2):
            arrived(chunk(fz.at[h], q), cz_recv.at[4 * h + q])
            go(chunk(fz.at[h], q), col_slot(e, x, q), cx_send.at[4 * h + q], cx_recv.at[4 * e + q], x_to[h])

    col_up, col_down, far_cols = {}, {}, []

    def cols_y(q):
        for e in range(2):
            mine = col_slot(e, entry_x(y, e), q)
            arrived(mine, cx_recv.at[4 * e + q])
            col_up[e, q] = net.put(mine, mine, yp)
            col_down[e, q] = net.put(mine, mine, ym)

    def cols_forward(q):
        for e in range(2):
            first, neighbour, where = (col_down[e, q], (y + 1) % 4, ym) if q % 2 else (col_up[e, q], (y + 3) % 4, yp)
            first.wait_recv()
            passed = col_slot(e, entry_x(neighbour, e), q)
            far_cols.append(net.put(passed, passed, where))

    for q in range(4):
        cols_z(q)
    rings[0].forward()
    next_slab(1)
    cols_x(0)
    cols_x(1)
    cols_y(0)
    cols_x(2)
    cols_y(1)
    cols_x(3)
    rings[1].forward()
    next_slab(2)
    cols_y(2)
    cols_forward(0)
    cols_y(3)
    cols_forward(1)
    next_slab(3)
    rings[2].forward()
    cols_forward(2)
    cols_forward(3)
    rings[3].forward()
    load_start.wait()
    for p in range(PARTS):
        x0[p] = x0f[:, W * p : W * (p + 1)].astype(BF16)
    for e in range(2):
        for q in range(4):
            (col_up if q % 2 else col_down)[e, q].wait_recv()
    for copy in far_cols:
        copy.wait_recv()

    load_green.wait()
    load_fock.wait()
    own.wait()

    def sig_copy(u):
        return pltpu.make_async_remote_copy(
            src_ref=sgs.at[u], dst_ref=sgr.at[u], send_sem=sig_send.at[u], recv_sem=sig_recv.at[u],
            device_id=other, device_id_type=pl.DeviceIdType.MESH,
        )

    def slab_sigma(slab):
        row0 = pl.multiple_of(SLAB * slab, 128)

        @pl.loop(0, BLOCK // TILE)
        def _(j):
            col0 = pl.multiple_of(TILE * j, TILE)
            total = jnp.zeros((SLAB, TILE), F32)
            for p in range(2):
                product = lax.dot_general(
                    frow[p, pl.ds(row0, SLAB), :], fcol[p, pl.ds(col0, TILE), :], NT, preferred_element_type=F32
                )
                total = total + product * grn[p, pl.ds(row0, SLAB), pl.ds(col0, TILE)].astype(F32)
            bands = []
            for b in range(SLAB // 128):
                keep = mask[6 * r + (3 * slab + b) // 2, 3 * c + j].astype(F32)
                bands.append(total[128 * b : 128 * (b + 1)] * keep)
            kept = jnp.concatenate(bands, axis=0)

            @pl.when(slab // 2 == t)
            def _():
                sig[slab % 2, :, pl.ds(col0, TILE)] = kept

            @pl.when(slab // 2 != t)
            def _():
                sgs[slab % 2, :, pl.ds(col0, TILE)] = kept.astype(BF16)

        @pl.when(slab // 2 != t)
        def _():
            sig_copy(slab % 2).start()

    center = 0.5 * (upper[0] + lower[0])
    half_width = 0.5 * (upper[0] - lower[0])

    def make_operator(which):
        for slab in which:
            u = slab % 2
            sig_copy(u).wait_recv()
            rows = pl.ds(pl.multiple_of(SLAB * u, 128), SLAB)
            shifted = fck[rows, :].astype(F32) + (sig[u] + sgr[u].astype(F32))
            row_ids = lax.broadcasted_iota(jnp.int32, (SLAB, BLOCK), 0) + (2 * BLOCK * r + SLAB * slab)
            col_ids = lax.broadcasted_iota(jnp.int32, (SLAB, BLOCK), 1) + BLOCK * c
            shifted = jnp.where(row_ids == col_ids, shifted - center, shifted)
            op[rows, :] = (shifted / half_width).astype(BF16)

    rings[0].finish()
    slab_sigma(slabs[0])
    rings[1].finish()
    slab_sigma(slabs[1])
    pl.when(zl // 2 == t)(lambda: make_operator(slabs[:2]))
    rings[2].finish()
    slab_sigma(slabs[2])
    rings[3].finish()
    slab_sigma(slabs[3])
    pl.when(zl // 2 != t)(lambda: make_operator(slabs[2:]))

    def direct_reduce(me, plus, minus, opposite, size, ready, part, stage, near, far):
        def rows(i):
            return pl.ds(pl.multiple_of(size * i, 32), size)

        copies = []
        for k, where, into in ((2, opposite, far), (1, plus, near.at[0]), (3, minus, near.at[1])):
            at = rows((me + k) % 4)
            ready((me + k) % 4)
            stage[at, :] = part[at, :].astype(BF16)
            copies.append(net.put(stage.at[at, :], into, where))
        ready(me)
        yield
        for copy in copies:
            copy.wait_recv()
        at = rows(me)
        part[at, :] = part[at, :] + far[...].astype(F32) + (near[0].astype(F32) + near[1].astype(F32))

    def ring_reduce(me, plus, minus, size, ready, part, stage, near, far):
        h = size // 2

        def rows(i, half):
            return pl.ds(pl.multiple_of(size * i + h * half, 16), h)

        def push(i, half, there, where):
            return net.put(stage.at[rows(i, half), :], there, where)

        a, b, opposite = (me + 1) % 4, (me + 3) % 4, (me + 2) % 4
        ready(opposite)
        for half in range(2):
            stage[rows(opposite, half), :] = part[rows(opposite, half), :].astype(BF16)
        far_up = push(opposite, 0, far.at[0], plus)
        far_down = push(opposite, 1, far.at[1], minus)
        ready(a)
        stage[rows(a, 1), :] = part[rows(a, 1), :].astype(BF16)
        up1 = push(a, 1, near.at[1], plus)
        ready(b)
        stage[rows(b, 0), :] = part[rows(b, 0), :].astype(BF16)
        down0 = push(b, 0, near.at[2], minus)
        ready(me)
        yield
        far_up.wait_recv()
        stage[rows(a, 0), :] = (part[rows(a, 0), :] + far[0].astype(F32)).astype(BF16)
        up0 = push(a, 0, near.at[0], plus)
        far_down.wait_recv()
        stage[rows(b, 1), :] = (part[rows(b, 1), :] + far[1].astype(F32)).astype(BF16)
        down1 = push(b, 1, near.at[3], minus)
        yield
        for copy in (up1, down0, up0, down1):
            copy.wait_recv()
        for half in range(2):
            at = rows(me, half)
            part[at, :] = part[at, :] + near[half].astype(F32) + near[2 + half].astype(F32)

    def across(block, n, p):
        prt = part.at[p]

        def ready(i):
            at = pl.ds(pl.multiple_of(QUARTER * i, 64), QUARTER)
            prt[at, :] = jnp.dot(op[at, :], block[...], preferred_element_type=F32)

        k = PARTS * n + p
        yield from ring_reduce(x, xp, xm, QUARTER, ready, prt, stage.at[k], near.at[k], far.at[k])
        zout[k] = prt[pl.ds(pl.multiple_of(QUARTER * x, 64), QUARTER), :].astype(BF16)

        def share(s):
            return pl.ds(pl.multiple_of(SHARE * s, 16), SHARE)

        copies = [net.put(zout.at[k, share(zls[d]), :], zin.at[k, d - 1], zdev[d]) for d in (1, 2, 3)]
        yield
        total = prt[pl.ds(pl.multiple_of(QUARTER * x + SHARE * zl, 16), SHARE), :]
        for d in (1, 2, 3):
            copies[d - 1].wait_recv()
            total = total + zin[k, d - 1].astype(F32)
        return total

    def gather_rows(buffer, complete=lambda i: None):
        def slots(s):
            def slot(i, half=None):
                rows = pl.ds(pl.multiple_of(QUARTER * i + SHARE * s, 16), SHARE)
                return buffer.at[rows, :] if half is None else buffer.at[rows, pl.ds(W // 2 * half, W // 2)]
            return slot

        here = slots(zl)(x)
        zc = [net.put(here, here, zdev[d]) for d in (1, 2, 3)]
        rings = [RingGather(net, x, xp, xm, slots(zl))]
        yield
        for d in (1, 2, 3):
            zc[d - 1].wait_recv()
            rings.append(RingGather(net, x, xp, xm, slots(zls[d])))
        complete(x)
        yield
        for ring in rings:
            ring.forward()
        complete((x + 3) % 4)
        complete((x + 1) % 4)
        yield
        for ring in rings:
            ring.finish()
        complete((x + 2) % 4)

    far_half = pl.ds(pl.multiple_of(SLAB * (1 - t), SLAB), SLAB)
    near_half = pl.ds(pl.multiple_of(SLAB * t, SLAB), SLAB)
    rows_o = pl.ds(pl.multiple_of(BLOCK * (1 - t), BLOCK), BLOCK)
    my_share = pl.ds(pl.multiple_of(QUARTER * x + SHARE * zl, 16), SHARE)
    my_out = pl.ds(pl.multiple_of(BLOCK * t + QUARTER * x + SHARE * zl, 16), SHARE)
    shard = SLAB // 4
    my_shard = pl.ds(pl.multiple_of(shard * y, 32), shard)
    mine2 = pl.ds(pl.multiple_of(SLAB * t + shard * y, 32), shard)
    stores = []

    def transpose():
        yield
        for i in range(3):
            for j in range(3):
                opt[pl.ds(TILE * j, TILE), pl.ds(TILE * i, TILE)] = op[pl.ds(TILE * i, TILE), pl.ds(TILE * j, TILE)].T

    def steps(p):
        cols = pl.ds(W * p, W)
        total = yield from across(x0.at[p], 0, p)
        y1own[p] = total
        y1[p, my_share, :] = total.astype(BF16)
        yield from gather_rows(y1.at[p])

        cstage[p] = jnp.dot(opt[far_half, :], y1[p], preferred_element_type=F32).astype(BF16)
        swap = net.put(cstage.at[p], cin.at[p], other)
        part2[p] = jnp.dot(opt[near_half, :], y1[p], preferred_element_type=F32)
        yield
        swap.wait_recv()
        part2[p] = part2[p] + cin[p].astype(F32)
        yield from direct_reduce(
            y, yp, ym, yo, shard, lambda i: None, part2.at[p], stage2.at[p], near2.at[p], far2.at[p]
        )
        hout[p] = part2[p, my_shard, :].astype(BF16)
        over = net.put(hout.at[p], hin.at[p], hdev)
        yield
        over.wait_recv()
        total = part2[p, my_shard, :] + hin[p].astype(F32)

        def slot2(i, half=None):
            rows = pl.ds(pl.multiple_of(SLAB * t + shard * i, 32), shard)
            return y2.at[p, rows, :] if half is None else y2.at[p, rows, pl.ds(W // 2 * half, W // 2)]

        y2[p, mine2, :] = (2.0 * total - x0f[mine2, cols]).astype(BF16)
        ring = DirectGather(net, y, yp, ym, yo, slot2)
        yield
        both = [net.put(slot2(y), slot2(y), other)]
        for copy, i in zip(ring.copies[1:] + ring.copies[:1], (y + 3, y + 1, y + 2)):
            copy.wait_recv()
            both.append(net.put(slot2(i % 4), slot2(i % 4), other))
        yield
        for copy in both:
            copy.wait_recv()

        total = yield from across(y2.at[p], 1, p)
        y3[p, my_out, :] = (2.0 * total - y1own[p]).astype(BF16)
        last = []

        def pass_on(i):
            quarter = y3.at[p, pl.ds(pl.multiple_of(BLOCK * t + QUARTER * i, 64), QUARTER), :]
            last.append(net.put(quarter, quarter, other))

        yield from gather_rows(y3.at[p, rows_t, :], pass_on)
        stores.append(pltpu.make_async_copy(y3.at[p, rows_t, :], out.at[rows_t, cols], local.at[4 + 2 * p]))
        stores[-1].start()
        yield
        for copy in last:
            copy.wait_recv()
        stores.append(pltpu.make_async_copy(y3.at[p, rows_o, :], out.at[rows_o, cols], local.at[5 + 2 * p]))
        stores[-1].start()

    in_turn(*[steps(p) for p in range(PARTS)], transpose())

    for copy in sends:
        copy.wait_send()
    for condition, copy in z_sent:
        pl.when(condition)(lambda: copy.wait_send())
    for u in range(2):
        sig_copy(u).wait_send()
    net.drain()
    for copy in stores:
        copy.wait()


def on_device(fock, green, factors, tile_mask, start_block, lower_edge, upper_edge):
    anywhere, smem = pl.BlockSpec(memory_space=pl.ANY), pl.BlockSpec(memory_space=pltpu.SMEM)
    v, dma = pltpu.VMEM, pltpu.SemaphoreType.DMA
    q2, s2 = QUARTER // 2, SLAB // 8
    result = pl.pallas_call(
        kernel,
        out_shape=jax.ShapeDtypeStruct((2 * BLOCK, SUB), BF16),
        in_specs=[anywhere] * 4 + [smem] * 3,
        out_specs=anywhere,
        scratch_shapes=[
            v((2, 2 * BLOCK, 768), BF16),
            v((2, BLOCK, 768), BF16),
            v((2, PIECE, 768), BF16),
            v((2, 2, PIECE, 768), BF16),
            v((2, 2 * BLOCK, BLOCK), BF16),
            v((BLOCK, BLOCK), BF16),
            v((BLOCK, SUB), F32),
            v((PARTS, BLOCK, W), BF16),
            v((2, SLAB, BLOCK), F32),
            v((2, SLAB, BLOCK), BF16),
            v((2, SLAB, BLOCK), BF16),
            v((BLOCK, BLOCK), BF16),
            v((BLOCK, BLOCK), BF16),
            v((PARTS, BLOCK, W), F32),
            v((2 * PARTS, BLOCK, W), BF16),
            v((2 * PARTS, 4, q2, W), BF16),
            v((2 * PARTS, 2, q2, W), BF16),
            v((2 * PARTS, 3, SHARE, W), BF16),
            v((2 * PARTS, QUARTER, W), BF16),
            v((PARTS, BLOCK, W), BF16),
            v((PARTS, SHARE, W), F32),
            v((PARTS, SLAB, W), F32),
            v((PARTS, SLAB, W), BF16),
            v((PARTS, SLAB, W), BF16),
            v((PARTS, SLAB, W), BF16),
            v((PARTS, 2, 2 * s2, W), BF16),
            v((PARTS, 2 * s2, W), BF16),
            v((PARTS, 2 * s2, W), BF16),
            v((PARTS, 2 * s2, W), BF16),
            v((PARTS, BLOCK, W), BF16),
            v((PARTS, 2 * BLOCK, W), BF16),
            dma((COPIES,)),
            dma((COPIES,)),
            dma((5,)),
            dma((4,)),
            dma((4,)),
            dma((4,)),
            dma((8,)),
            dma((8,)),
            dma((8,)),
            dma((8,)),
            dma((2,)),
            dma((2,)),
            dma((4 + 2 * PARTS,)),
        ],
        compiler_params=pltpu.CompilerParams(
            collective_id=0, has_side_effects=True, vmem_limit_bytes=52 * 2**20
        ),
        name="filter_kernel",
    )(factors, green, fock, start_block, tile_mask, lower_edge, upper_edge)
    return result.astype(F32)


def solution(mesh):
    placed = (
        P("row", "col"),
        P("tau", "row", "col"),
        P("tau", ("row", "col"), None),
        P(),
        P("col", None),
        P(),
        P(),
    )
    return jax.shard_map(
        on_device, mesh=mesh, in_specs=placed, out_specs=P("row", None), check_vma=False
    )
```
